32 devices in a mesh: clip: 16 (over z, x, core), val: 2 (over y).
Axes of the slice: x: 2, y: 2, z: 4, core: 2. Of those that a mesh axis runs over, the one named last changes fastest.
Arguments:
- latents: bfloat16 [256, 8192], P('clip', 'val'), may hold values from -10 to 10
- noise: bfloat16 [256, 8192], P('clip', 'val'), may hold values from -10 to 10
- offsets: int32 [256, 2, 2], P('clip'), may hold values from 0 to 15
- times: float32 [256], P('clip'), may hold values from 0.05 to 0.95
- embed: bfloat16 [64, 5120], replicated, may hold values from -0.75 to 0.75
Outputs:
- embedded: bfloat16 [256, 128, 5120], P('clip', 'val')
The draws below stay inside these ranges and needn't reach their ends.
All inputs are finite; a program needn't handle non-finite values.
Results may differ from the reference program's by a relative error of at most 0.0051.
Values may be sent and summed in bfloat16 or wider, within the bound.
No kernel may reach another device: no remote copies, remote signals or barrier semaphores. Data moves between devices by JAX's collectives and lax.ppermute only.
A program may use at most 64 MiB of HBM per device.

```python
import math
import jax
import jax.numpy as jnp
from jax import lax

P_SIZE = 64
D = 5120
FR = 2
GW = 16
GH = 4
ITERS = 4
S = 128
N = 256


def frame_pattern(key, strength_index):
    local_key = jax.random.fold_in(key, 100 + strength_index)
    root_three = math.sqrt(3.0)
    pattern = jax.random.uniform(local_key, (P_SIZE, FR, 1), jnp.float32, -root_three, root_three)
    return jnp.broadcast_to(pattern, (P_SIZE, FR, GH * GW)).reshape(P_SIZE * FR * GH * GW)


def pattern_scale(strength_index):
    target = 150.0 * (strength_index + 1)
    return math.sqrt(target / (2.0 * math.sqrt(P_SIZE * FR * GH * GW)))


def base_rows(key, salt):
    local_key = jax.random.fold_in(key, salt)
    values = jnp.clip(jax.random.normal(local_key, (N, P_SIZE * FR * GH * GW), jnp.float32), -6.0, 6.0)
    return values


def heavy_rows(key):
    local_key = jax.random.fold_in(key, 300)
    values = jnp.clip(3.0 * jax.random.normal(local_key, (2, P_SIZE * FR * GH * GW), jnp.float32), -10.0, 10.0)
    return values


def draw_latents(key, part):
    values = base_rows(key, 1)
    for strength_index in range(3):
        pattern = frame_pattern(key, strength_index)
        values = values.at[strength_index].set(pattern_scale(strength_index) * pattern)
    return values.astype(jnp.bfloat16)


def draw_noise(key, part):
    values = base_rows(key, 2)
    for strength_index in range(3):
        pattern = frame_pattern(key, strength_index)
        scale = pattern_scale(strength_index)
        values = values.at[N - 1 - 2 * strength_index].set(scale * pattern)
        values = values.at[N - 2 - 2 * strength_index].set(1.08 * scale * pattern)
    heavy = heavy_rows(key)
    values = values.at[N // 2 - 2].set(heavy[0])
    values = values.at[N // 2 - 1].set(heavy[1])
    return values.astype(jnp.bfloat16)


def set_ends(values, rng, least, largest):
    longest = values.shape.index(max(values.shape))
    spots = []
    for shift in (0, 1):
        where = [jax.random.randint(jax.random.fold_in(rng, axis), (), 0, length) for axis, length in enumerate(values.shape)]
        where[longest] = (where[longest] + shift) % values.shape[longest]
        spots.append(tuple(where))
    return values.at[spots[0]].set(least).at[spots[1]].set(largest)


def levels(stream_key, shape, split, smallest, high):
    def one(dim, parts):
        steps = jax.random.uniform(jax.random.fold_in(jax.random.fold_in(stream_key, 6), dim), (parts,), jnp.float32, smallest / len(split), high / len(split))
        return jnp.repeat(jnp.exp(steps), shape[dim] // parts).reshape((-1,) + (1,) * (len(shape) - dim - 1))

    loudness = one(*split[0])
    for cut in split[1:]:
        loudness = loudness * one(*cut)
    return loudness


def gaussian(stream_key, dims, spread, limit, kind=jnp.bfloat16):
    entries = jax.random.normal(stream_key, dims, jnp.float32) * spread
    return jnp.minimum(jnp.maximum(entries, -limit), limit).astype(kind)


def setup_inputs(seed: int = 0) -> dict:
    key_of = jax.random.split(jax.random.key(seed), 6)
    latents = draw_latents(jax.random.fold_in(key_of[5], 71), 0)
    noise = draw_noise(jax.random.fold_in(key_of[5], 71), 0)
    offsets = set_ends(jax.random.randint(key_of[2], (N, FR, 2), 0, GW), jax.random.fold_in(key_of[2], 1), 0, GW - 1).astype(jnp.int32)
    times = jnp.clip(0.05 + 0.9 * jax.random.uniform(key_of[3], (N,), jnp.float32) ** levels(key_of[3], (N,), ((0, 16),), -0.2, 0.2), 0.05, 0.95)
    embed = gaussian(key_of[4], (P_SIZE, D), P_SIZE ** -0.5, 0.75)
    return {"latents": latents, "noise": noise, "offsets": offsets, "times": times, "embed": embed}


def warp_noise(noise, offsets):
    clips = noise.shape[0]
    tokens = FR * GH * GW
    value_cube = noise.reshape(clips, noise.shape[1] // tokens, tokens)
    shift_y = offsets[:, :, 0] % GH
    shift_x = offsets[:, :, 1] % GW
    src_rows = (jnp.arange(GH, dtype=jnp.int32)[None, None, :] - shift_y[:, :, None]) % GH
    src_cols = (jnp.arange(GW, dtype=jnp.int32)[None, None, :] - shift_x[:, :, None]) % GW
    frame_base = (jnp.arange(FR, dtype=jnp.int32) * (GH * GW))[None, :, None, None]
    source = (frame_base + src_rows[:, :, :, None] * GW + src_cols[:, :, None, :]).reshape(clips, tokens).astype(jnp.int32)
    source = jnp.broadcast_to(source[:, None, :], value_cube.shape)
    return jnp.take_along_axis(value_cube, source, axis=2).reshape(noise.shape)

def log_sum_exp(values, axis):
    top = lax.optimization_barrier(jnp.max(values, axis=axis, keepdims=True))
    return jnp.squeeze(top + jnp.log(lax.optimization_barrier(jnp.sum(jnp.exp(values - top), axis=axis, keepdims=True))), axis=axis)

def embed_clip(single, embed):
    return jnp.dot(single.T, embed, preferred_element_type=jnp.float32).astype(jnp.bfloat16)

def reference(latents, noise, offsets, times, embed):
    warped = warp_noise(noise, offsets)
    square = lax.optimization_barrier(jnp.sum(jnp.square(warped.astype(jnp.float32)), axis=1))
    gram = jnp.dot(latents, warped.T, preferred_element_type=jnp.float32)
    volume = P_SIZE * S
    cost = (square[None, :] - 2.0 * gram) / volume
    entropy = 0.5 / math.sqrt(volume)
    column_dual = jnp.zeros((N,), jnp.float32)
    for sweep_index in range(ITERS):
        row_dual = -entropy * log_sum_exp((column_dual[None, :] - cost) / entropy, 1)
        column_dual = -entropy * log_sum_exp((row_dual[:, None] - cost) / entropy, 0)
    scores = (column_dual[None, :] - cost) / entropy
    top = lax.optimization_barrier(jnp.max(scores, axis=1, keepdims=True))
    expo = jnp.exp(scores - top)
    weights = (expo / lax.optimization_barrier(jnp.sum(expo, axis=1, keepdims=True))).astype(jnp.bfloat16)
    coupled = jnp.dot(weights, warped, preferred_element_type=jnp.float32)
    mixed = ((1.0 - times)[:, None] * latents.astype(jnp.float32) + times[:, None] * coupled).astype(jnp.bfloat16)
    value_cube = mixed.reshape(N, P_SIZE, S)
    return lax.map(lambda single: embed_clip(single, embed), value_cube)
```

```python
import functools
import math

import jax
import jax.numpy as jnp
from jax import lax
from jax.experimental import pallas as pl
from jax.experimental.pallas import tpu as pltpu
from jax.sharding import PartitionSpec as P

P_SIZE = 64
D = 5120
FR = 2
GW = 16
GH = 4
ITERS = 4
S = 128
FRAME = GW * GH
SCALE = 2.0 / math.sqrt(P_SIZE * S)
NT = (((1,), (1,)), ((), ()))
TN = (((0,), (0,)), ((), ()))
F32 = jnp.float32
BF16 = jnp.bfloat16
ANY = pl.BlockSpec(memory_space=pl.ANY)
VMEM = pl.BlockSpec(memory_space=pltpu.VMEM)
SMEM = pl.BlockSpec(memory_space=pltpu.SMEM)


def params():
    return pltpu.CompilerParams(vmem_limit_bytes=48 * 1024 * 1024)


def warp_kernel(offsets, noise, out):
    clips, values = noise.shape
    row = lax.broadcasted_iota(jnp.int32, (clips, S), 0)
    token = lax.broadcasted_iota(jnp.int32, (clips, S), 1)
    frame = token // FRAME
    shift_y = jnp.zeros((clips, S), jnp.int32)
    shift_x = jnp.zeros((clips, S), jnp.int32)
    for i in range(clips):
        for f in range(FR):
            here = (row == i) & (frame == f)
            shift_y = jnp.where(here, offsets[i, f * 2], shift_y)
            shift_x = jnp.where(here, offsets[i, f * 2 + 1], shift_x)
    src_row = ((token // GW) - shift_y) & (GH - 1)
    src_col = (token - shift_x) & (GW - 1)
    source = frame * FRAME + src_row * GW + src_col
    for p in range(values // S):
        tile = noise[:, p * S : (p + 1) * S].astype(F32)
        moved = jnp.take_along_axis(tile, source, axis=1, mode="promise_in_bounds")
        out[:, p * S : (p + 1) * S] = moved.astype(BF16)


def warp_noise(noise, offsets):
    clips = noise.shape[0]
    return pl.pallas_call(
        warp_kernel,
        out_shape=jax.ShapeDtypeStruct(noise.shape, BF16),
        in_specs=[SMEM, VMEM],
        out_specs=VMEM,
        compiler_params=params(),
        name="warp",
    )(offsets.reshape(clips, FR * 2), noise)


def gram_kernel(clips, outer, inner, *refs):
    lat = refs[:inner]
    noi = refs[inner : inner + outer]
    out, held, sems = refs[inner + outer :]
    place = lax.axis_index("clip")
    a, b = place // inner, place % inner
    rows = clips * inner
    copies = []
    for k in range(inner):
        at = pl.multiple_of((b ^ k) * clips, clips)
        copies.append(pltpu.make_async_copy(lat[k], held.at[pl.ds(at, clips)], sems.at[k]))
    for s in range(outer):
        at = pl.multiple_of(rows + ((a + outer - s) % outer) * clips, clips)
        copies.append(pltpu.make_async_copy(noi[s], held.at[pl.ds(at, clips)], sems.at[inner + s]))
    for c in copies:
        c.start()
    for c in copies:
        c.wait()
    both = held[...]
    cols = clips * outer
    prod = lax.dot_general(both, both[rows:], NT, preferred_element_type=F32)
    inner_prod, own = prod[:rows], prod[rows:]
    eye = lax.broadcasted_iota(jnp.int32, (cols, cols), 0) == lax.broadcasted_iota(
        jnp.int32, (cols, cols), 1
    )
    square = jnp.sum(jnp.where(eye, own, 0.0), axis=0, keepdims=True)
    part = square - 2.0 * inner_prod
    out[...] = jnp.concatenate([part[: rows // 2], part[rows // 2 :]], axis=1)


def gram_block(lat, noi):
    clips, values = lat[0].shape
    inner, outer = len(lat), len(noi)
    return pl.pallas_call(
        functools.partial(gram_kernel, clips, outer, inner),
        out_shape=jax.ShapeDtypeStruct((clips * inner // 2, clips * outer * 2), F32),
        in_specs=[ANY] * (inner + outer),
        out_specs=VMEM,
        scratch_shapes=[
            pltpu.VMEM((clips * (inner + outer), values), BF16),
            pltpu.SemaphoreType.DMA((inner + outer,)),
        ],
        compiler_params=params(),
        name="gram",
    )(*lat, *noi)


def sinkhorn(kernel, own):
    col = jnp.zeros((1, kernel.shape[1]), F32)
    for _ in range(ITERS):
        u = kernel + col
        top = jnp.max(u, axis=1, keepdims=True)
        row = -(top + jnp.log(jnp.sum(jnp.exp(u - top), axis=1, keepdims=True)))
        u = kernel + row
        top = jnp.max(u, axis=0, keepdims=True)
        col = -(top + jnp.log(jnp.sum(jnp.exp(u - top), axis=0, keepdims=True)))
    u = own + col
    top = jnp.max(u, axis=1, keepdims=True)
    e = jnp.exp(u - top)
    return (e / jnp.sum(e, axis=1, keepdims=True)).astype(BF16)


def plan_kernel(clips, outer, *refs):
    mine, other = refs[:outer], refs[outer : 2 * outer]
    out, full = refs[2 * outer :]
    place = lax.axis_index("clip")
    inner = 4
    b = place % inner
    half = mine[0].shape[0] // 2
    low = lax.broadcasted_iota(jnp.int32, (half, 128), 1) < 64
    for s in range(outer):
        for x in range(2):
            g = mine[s][x * half : (x + 1) * half, :] * (-SCALE)
            h = other[s][x * half : (x + 1) * half, :] * (-SCALE)
            lanes = slice(x * 128, (x + 1) * 128)
            r = s * 2 * half
            full[r : r + half, lanes] = jnp.where(low, g, pltpu.roll(h, 64, 1))
            full[r + half : r + 2 * half, lanes] = jnp.where(low, pltpu.roll(g, 64, 1), h)
    own = full[pl.ds(pl.multiple_of(b * clips, clips), clips), :]
    out[...] = sinkhorn(full[...], own)


def plan(mine, other, clips):
    outer = len(mine)
    n = 256
    return pl.pallas_call(
        functools.partial(plan_kernel, clips, outer),
        out_shape=jax.ShapeDtypeStruct((clips, n), BF16),
        in_specs=[VMEM] * (2 * outer),
        out_specs=VMEM,
        scratch_shapes=[pltpu.VMEM((n, n), F32)],
        compiler_params=params(),
        name="plan",
    )(*mine, *other)


def mix_kernel(clips, outer, groups, times, weights, latents, *refs):
    parts = refs[:groups]
    keep, send, panel, cube, sems = refs[groups:]
    place = lax.axis_index("clip")
    val = lax.axis_index("val")
    inner = 4
    a = place // inner
    copies = []
    for g in range(groups):
        for s in range(outer):
            at = pl.multiple_of((g * outer + (a + outer - s) % outer) * clips, clips)
            copies.append(
                pltpu.make_async_copy(
                    parts[g].at[pl.ds(s * clips, clips)],
                    panel.at[pl.ds(at, clips)],
                    sems.at[g * outer + s],
                )
            )
    for c in copies:
        c.start()
    row = lax.broadcasted_iota(jnp.int32, (clips, 1), 0)
    t = jnp.zeros((clips, 1), F32)
    for i in range(clips):
        t = jnp.where(row == i, times[i], t)
    for c in copies:
        c.wait()
    w = weights[...]
    values = latents.shape[1]
    patch = values // S
    step = 512
    for at in range(0, values, step):
        coupled = jnp.dot(w, panel[:, at : at + step], preferred_element_type=F32)
        mixed = (1.0 - t) * latents[:, at : at + step].astype(F32) + t * coupled
        for q in range(step // S):
            cube[:, at // S + q, :] = mixed[:, q * S : (q + 1) * S]
    low = lax.broadcasted_iota(jnp.int32, (patch, S), 1) < FRAME
    for i in range(0, clips, 2):
        x, y = cube[i], cube[i + 1]
        first = jnp.where(low, x, pltpu.roll(y, FRAME, 1))
        second = jnp.where(low, pltpu.roll(x, FRAME, 1), y)
        lanes = slice(i * FRAME, (i + 2) * FRAME)
        keep[:, lanes] = jnp.where(val == 0, first, second).astype(BF16)
        send[:, lanes] = jnp.where(val == 0, second, first).astype(BF16)


def mix(times, weights, latents, parts, outer):
    clips, values = latents.shape
    groups = len(parts)
    patch = values // S
    shape = jax.ShapeDtypeStruct((patch, clips * FRAME), BF16)
    return pl.pallas_call(
        functools.partial(mix_kernel, clips, outer, groups),
        out_shape=[shape, shape],
        in_specs=[SMEM, VMEM, VMEM] + [ANY] * groups,
        out_specs=[VMEM, VMEM],
        scratch_shapes=[
            pltpu.VMEM((clips * outer * groups, values), BF16),
            pltpu.VMEM((clips, patch, S), F32),
            pltpu.SemaphoreType.DMA((groups * outer,)),
        ],
        compiler_params=params(),
        name="mix",
    )(times, weights, latents, *parts)


def embed_kernel(keep, got, embed, out):
    first = lax.axis_index("val") == 0
    k, g = keep[...], got[...]
    lhs = jnp.concatenate([jnp.where(first, k, g), jnp.where(first, g, k)], axis=0)
    out[...] = lax.dot_general(lhs, embed[...], TN, preferred_element_type=F32).astype(BF16)


def embed_tokens(keep, got, embed):
    patch, tokens = keep.shape
    block = 128
    return pl.pallas_call(
        embed_kernel,
        grid=(tokens // block,),
        out_shape=jax.ShapeDtypeStruct((tokens, embed.shape[1]), BF16),
        in_specs=[
            pl.BlockSpec((patch, block), lambda i: (0, i)),
            pl.BlockSpec((patch, block), lambda i: (0, i)),
            pl.BlockSpec(embed.shape, lambda i: (0, 0)),
        ],
        out_specs=pl.BlockSpec((block, embed.shape[1]), lambda i: (i, 0)),
        compiler_params=params(),
        name="embed",
    )(keep, got, embed)


def flip(n, bit):
    return [(i, i ^ bit) for i in range(n)]


def on_device(n, latents, noise, offsets, times, embed):
    clips = latents.shape[0]
    outer, inner = n // 4, 4

    def core(x):
        return lax.ppermute(x, "clip", flip(n, 1))

    def across(x):
        return lax.ppermute(x, "clip", flip(n, 2))

    def along(x, s):
        hop = [(i, (i + s * inner) % n) for i in range(n)]
        return lax.ppermute(x, "clip", hop)

    def other_val(x):
        return lax.ppermute(x, "val", [(0, 1), (1, 0)])

    def other_both(x):
        pairs = [(2 * i + v, 2 * (i ^ 2) + 1 - v) for i in range(n) for v in range(2)]
        return lax.ppermute(x, ("clip", "val"), pairs)

    warped = warp_noise(noise, offsets)
    lat_x = across(latents)
    lat = [latents, core(latents), lat_x, core(lat_x)]
    noi = [warped] + [along(warped, s) for s in range(1, outer)]
    part = gram_block(lat, noi)
    got_x, got_v, got_b = across(part), other_val(part), other_both(part)
    pair = jnp.concatenate([part + got_v, got_x + got_b], axis=0)
    mine = [pair] + [along(pair, s) for s in range(1, outer)]
    other = core(jnp.concatenate(mine, axis=0))
    rows = pair.shape[0]
    other = [other[s * rows : (s + 1) * rows] for s in range(outer)]
    line = jnp.concatenate(noi, axis=0)
    line_x = across(line)
    parts = [line, core(line), line_x, core(line_x)]
    weights = plan(mine, other, clips)
    keep, send = mix(times, weights, latents, parts, outer)
    out = embed_tokens(keep, other_val(send), embed)
    return out.reshape(clips, FRAME, embed.shape[1])


def warp_and_gather(latents, noise, offsets, times, embed):
    clips = latents.shape[0]
    warped = warp_noise(noise, offsets)
    panel = lax.all_gather(warped, "clip", axis=0, tiled=True)
    gram = lax.dot_general(latents, panel, NT, preferred_element_type=F32)
    square = jnp.sum(jnp.square(panel.astype(F32)), axis=1)
    part = lax.psum(square[None, :] - 2.0 * gram, "val")
    full = lax.all_gather(part, "clip", axis=0, tiled=True) * (-SCALE)
    weights = sinkhorn(full, part * (-SCALE))
    coupled = jnp.dot(weights, panel, preferred_element_type=F32)
    t = times[:, None]
    mixed = ((1.0 - t) * latents.astype(F32) + t * coupled).astype(BF16)
    cube = mixed.reshape(clips, latents.shape[1] // S, S)
    cube = lax.all_to_all(cube, "val", split_axis=2, concat_axis=1, tiled=True)
    return jnp.einsum("cps,pd->csd", cube, embed, preferred_element_type=F32).astype(BF16)


def solution(mesh):
    n, v = mesh.shape["clip"], mesh.shape["val"]
    body = functools.partial(on_device, n) if (n, v) == (16, 2) else warp_and_gather
    placed = (P("clip", "val"), P("clip", "val"), P("clip", None, None), P("clip"), P())
    return jax.shard_map(
        body, mesh=mesh, in_specs=placed, out_specs=P("clip", "val", None), check_vma=False
    )
```

```python
import functools
import math

import jax
import jax.numpy as jnp
from jax import lax
from jax.experimental import pallas as pl
from jax.experimental.pallas import tpu as pltpu
from jax.sharding import PartitionSpec as P

P_SIZE = 64
D = 5120
FR = 2
GW = 16
GH = 4
ITERS = 4
S = 128
FRAME = GW * GH
SCALE = 2.0 / math.sqrt(P_SIZE * S)
NT = (((1,), (1,)), ((), ()))
TN = (((0,), (0,)), ((), ()))
F32 = jnp.float32
BF16 = jnp.bfloat16
HBM = pl.BlockSpec(memory_space=pltpu.HBM)
VMEM = pl.BlockSpec(memory_space=pltpu.VMEM)
SMEM = pl.BlockSpec(memory_space=pltpu.SMEM)


def params():
    return pltpu.CompilerParams(vmem_limit_bytes=48 * 1024 * 1024)


def lane_sources(offsets, frame, token, clips):
    square = (clips, clips)
    eye = lax.broadcasted_iota(jnp.int32, square, 0) == lax.broadcasted_iota(jnp.int32, square, 1)

    def column(k):
        spread = jnp.where(eye, jnp.broadcast_to(offsets[k : k + 1, :], square), 0)
        return jnp.sum(spread, axis=1, keepdims=True)

    shift_y = jnp.where(frame == 0, column(0), column(2))
    shift_x = jnp.where(frame == 0, column(1), column(3))
    src_row = ((token // GW) - shift_y) & (GH - 1)
    src_col = (token - shift_x) & (GW - 1)
    return frame * FRAME + src_row * GW + src_col


def gather_lanes(tile, source):
    return jnp.take_along_axis(tile, source, axis=1, mode="promise_in_bounds")


def warp_kernel(offsets, noise, out):
    clips, values = noise.shape
    lane = lax.broadcasted_iota(jnp.int32, (clips, S), 1)
    source = lane_sources(offsets, lane // FRAME, lane % FRAME, clips)
    for p in range(values // S):
        cut = slice(p * S, (p + 1) * S)
        out[:, cut] = gather_lanes(noise[:, cut].astype(F32), source).astype(BF16)


def flat_offsets(offsets):
    return offsets.transpose(1, 2, 0).reshape(FR * 2, offsets.shape[0])


def warp_noise(noise, offsets):
    return pl.pallas_call(
        warp_kernel,
        out_shape=jax.ShapeDtypeStruct(noise.shape, BF16),
        in_specs=[VMEM, VMEM],
        out_specs=VMEM,
        compiler_params=params(),
        name="warp",
    )(flat_offsets(offsets), noise)


def split_kernel(offsets, noise, latents, noise_keep, noise_send, lat_keep, lat_send):
    clips, values = noise.shape
    half = values // S // 2
    val = lax.axis_index("val")
    lane = lax.broadcasted_iota(jnp.int32, (clips, S), 1)
    low = lane < FRAME
    keep_from = lane_sources(offsets, val + lane * 0, lane % FRAME, clips)
    send_from = lane_sources(offsets, 1 - val + lane * 0, lane % FRAME, clips)
    for q in range(half):
        near, far = slice(q * S, (q + 1) * S), slice((q + half) * S, (q + half + 1) * S)
        a, b = noise[:, near].astype(F32), noise[:, far].astype(F32)
        noise_keep[:, near] = jnp.where(
            low, gather_lanes(a, keep_from), gather_lanes(b, keep_from)
        ).astype(BF16)
        noise_send[:, near] = jnp.where(
            low, gather_lanes(a, send_from), gather_lanes(b, send_from)
        ).astype(BF16)
    for q in range(half):
        near, far = slice(q * S, (q + 1) * S), slice((q + half) * S, (q + half + 1) * S)
        a, b = latents[:, near].astype(F32), latents[:, far].astype(F32)
        first = jnp.where(low, a, pltpu.roll(b, FRAME, 1))
        second = jnp.where(low, pltpu.roll(a, FRAME, 1), b)
        lat_keep[:, near] = jnp.where(val == 0, first, second).astype(BF16)
        lat_send[:, near] = jnp.where(val == 0, second, first).astype(BF16)


def split_frames(noise, latents, offsets):
    clips, values = noise.shape
    shape = jax.ShapeDtypeStruct((clips, values // 2), BF16)
    return pl.pallas_call(
        split_kernel,
        out_shape=[shape] * 4,
        in_specs=[VMEM] * 3,
        out_specs=[VMEM] * 4,
        compiler_params=params(),
        name="split",
    )(flat_offsets(offsets), noise, latents)


def turn(x, by, lane):
    return jnp.where(lane % 64 >= by, pltpu.roll(x, by, 1), pltpu.roll(x, (by + 64) % 128, 1))


def gram_kernel(clips, lat_own, lat_core, noi_keep, noi_got, out):
    place = lax.axis_index("clip")
    a, x, c = place // 4, (place // 2) % 2, place % 2
    rows, cols = 4 * clips, noi_keep.shape[0]
    cut = noi_keep.shape[1]
    prod = jnp.zeros((rows + cols, cols), F32)
    for h, noi in enumerate((noi_keep, noi_got)):
        lanes = slice(h * cut, (h + 1) * cut)
        right = noi[...]
        left = jnp.concatenate([lat_own[:, lanes], lat_core[:, lanes], right], axis=0)
        prod += lax.dot_general(left, right, NT, preferred_element_type=F32)
    square = (cols, cols)
    eye = lax.broadcasted_iota(jnp.int32, square, 0) == lax.broadcasted_iota(jnp.int32, square, 1)
    norm = jnp.sum(jnp.where(eye, prod[rows:], 0.0), axis=0, keepdims=True)
    part = norm - 2.0 * prod[:rows]
    blocks = [part[k * clips : (k + 1) * clips] for k in range(4)]
    near0 = jnp.where(c == 0, blocks[0], blocks[2])
    near1 = jnp.where(c == 0, blocks[2], blocks[0])
    far0 = jnp.where(c == 0, blocks[1], blocks[3])
    far1 = jnp.where(c == 0, blocks[3], blocks[1])
    near = jnp.concatenate([near0, near1], axis=0)
    far = jnp.concatenate([far0, far1], axis=0)
    packed = jnp.concatenate([jnp.where(x == 0, near, far), jnp.where(x == 0, far, near)], axis=1)
    lane = lax.broadcasted_iota(jnp.int32, packed.shape, 1)
    out[...] = turn(packed, a * clips, lane)


def gram_block(clips, lat_own, lat_core, noi_keep, noi_got):
    return pl.pallas_call(
        functools.partial(gram_kernel, clips),
        out_shape=jax.ShapeDtypeStruct((2 * clips, 128), F32),
        in_specs=[VMEM] * 4,
        out_specs=VMEM,
        compiler_params=params(),
        name="gram",
    )(lat_own, lat_core, noi_keep, noi_got)


def sinkhorn(kernel, own):
    col = jnp.zeros((1, kernel.shape[1]), F32)
    for _ in range(ITERS):
        u = kernel + col
        top = jnp.max(u, axis=1, keepdims=True)
        row = -(top + jnp.log(jnp.sum(jnp.exp(u - top), axis=1, keepdims=True)))
        u = kernel + row
        top = jnp.max(u, axis=0, keepdims=True)
        col = -(top + jnp.log(jnp.sum(jnp.exp(u - top), axis=0, keepdims=True)))
    u = own + col
    top = jnp.max(u, axis=1, keepdims=True)
    e = jnp.exp(u - top)
    return e / jnp.sum(e, axis=1, keepdims=True)


def plan_kernel(clips, mine, other, out, full):
    place = lax.axis_index("clip")
    a, b = place // 4, place % 4
    half = 2 * clips
    low = lax.broadcasted_iota(jnp.int32, (half, 128), 1) < 64
    for s in range(mine.shape[0] // (2 * half)):
        for x in range(2):
            r = s * 2 * half
            g = mine[r + x * half : r + (x + 1) * half, :] * (-SCALE)
            h = other[r + x * half : r + (x + 1) * half, :] * (-SCALE)
            lanes = slice(x * 128, (x + 1) * 128)
            full[r : r + half, lanes] = jnp.where(low, g, pltpu.roll(h, 64, 1))
            full[r + half : r + 2 * half, lanes] = jnp.where(low, pltpu.roll(g, 64, 1), h)
    own = full[pl.ds(pl.multiple_of(b * clips, clips), clips), :]
    weights = sinkhorn(full[...], own)
    lane = lax.broadcasted_iota(jnp.int32, (clips, 128), 1)
    back = (4 - a) % 4 * clips
    for x in range(2):
        lanes = slice(x * 128, (x + 1) * 128)
        out[:, lanes] = turn(weights[:, lanes], back, lane).astype(BF16)


def plan(mine, other, clips):
    n = mine.shape[0]
    return pl.pallas_call(
        functools.partial(plan_kernel, clips),
        out_shape=jax.ShapeDtypeStruct((clips, n), BF16),
        in_specs=[VMEM] * 2,
        out_specs=VMEM,
        scratch_shapes=[pltpu.VMEM((n, n), F32)],
        compiler_params=params(),
        name="plan",
    )(mine, other)


def finish_kernel(clips, block, times, weights, lat, embed, *refs):
    keep, got = refs[:4], refs[4:8]
    out, cube, lhs, table, result, table_sem, sems = refs[8:]
    load = pltpu.make_async_copy(embed, table, table_sem)
    load.start()
    val = lax.axis_index("val")
    row = lax.broadcasted_iota(jnp.int32, (clips, 1), 0)
    t = jnp.zeros((clips, 1), F32)
    for i in range(clips):
        t = jnp.where(row == i, times[i], t)
    w = weights[...]
    cut = keep[0].shape[1]
    step = 256
    for h, parts in enumerate((keep, got)):
        for at in range(0, cut, step):
            panel = jnp.concatenate([p[:, at : at + step] for p in parts], axis=0)
            coupled = jnp.dot(w, panel, preferred_element_type=F32)
            here = h * cut + at
            mixed = (1.0 - t) * lat[:, here : here + step].astype(F32) + t * coupled
            for q in range(step // S):
                cube[:, here // S + q, :] = mixed[:, q * S : (q + 1) * S]
    tiles = 2 * cut // S
    half = tiles // 2
    low = lax.broadcasted_iota(jnp.int32, (tiles, S), 1) < FRAME
    for i in range(0, clips, 2):
        x, y = cube[i], cube[i + 1]
        near = jnp.where(low, x, pltpu.roll(y, FRAME, 1))
        far = jnp.where(low, pltpu.roll(x, FRAME, 1), y)
        mine = jnp.concatenate([near[:half], far[:half]], axis=0)
        other = jnp.concatenate([near[half:], far[half:]], axis=0)
        lanes = slice(i * FRAME, (i + 2) * FRAME)
        lhs[:tiles, lanes] = jnp.where(val == 0, mine, other).astype(BF16)
        lhs[tiles:, lanes] = jnp.where(val == 0, other, mine).astype(BF16)
    load.wait()
    tokens = lhs.shape[1]
    steps = tokens // block

    def store(k):
        at = pl.multiple_of(k * block, block)
        return pltpu.make_async_copy(result.at[k % 2], out.at[pl.ds(at, block)], sems.at[k % 2])

    for k in range(steps):
        if k >= 2:
            store(k - 2).wait()
        result[k % 2] = lax.dot_general(
            lhs[:, k * block : (k + 1) * block], table[...], TN, preferred_element_type=F32
        ).astype(BF16)
        store(k).start()
    for k in range(max(steps - 2, 0), steps):
        store(k).wait()


def finish(times, weights, lat, embed, keep, got, block=128):
    clips, values = lat.shape
    tokens, width = clips * FRAME, embed.shape[1]
    return pl.pallas_call(
        functools.partial(finish_kernel, clips, block),
        out_shape=jax.ShapeDtypeStruct((tokens, width), BF16),
        in_specs=[SMEM, VMEM, VMEM, HBM] + [VMEM] * 8,
        out_specs=HBM,
        scratch_shapes=[
            pltpu.VMEM((clips, values // S, S), F32),
            pltpu.VMEM((P_SIZE, tokens), BF16),
            pltpu.VMEM(embed.shape, BF16),
            pltpu.VMEM((2, block, width), BF16),
            pltpu.SemaphoreType.DMA,
            pltpu.SemaphoreType.DMA((2,)),
        ],
        compiler_params=params(),
        name="finish",
    )(times, weights, lat, embed, *keep, *got)


def flip(n, bit):
    return [(i, i ^ bit) for i in range(n)]


def on_device(n, latents, noise, offsets, times, embed):
    clips = latents.shape[0]
    outer, inner = n // 4, 4

    def core(x):
        return lax.ppermute(x, "clip", flip(n, 1))

    def across(x):
        return lax.ppermute(x, "clip", flip(n, 2))

    def along(x, s):
        hop = [((i + s * inner) % n, i) for i in range(n)]
        return lax.ppermute(x, "clip", hop)

    def line(x):
        return jnp.concatenate([x] + [along(x, s) for s in range(1, outer)], axis=0)

    def other_val(x):
        return lax.ppermute(x, "val", [(0, 1), (1, 0)])

    def other_both(x):
        pairs = [(2 * i + v, 2 * (i ^ 2) + 1 - v) for i in range(n) for v in range(2)]
        return lax.ppermute(x, ("clip", "val"), pairs)

    noi_keep, noi_send, lat_keep, lat_send = split_frames(noise, latents, offsets)
    noi_got = other_val(noi_send)
    keep_line = line(noi_keep)
    got_line = line(noi_got)
    lat = jnp.concatenate([lat_keep, other_val(lat_send)], axis=1)
    lat_own = jnp.concatenate([lat, across(lat)], axis=0)
    keep_across = across(keep_line)
    part = gram_block(clips, lat_own, core(lat_own), keep_line, got_line)
    got_x, got_v, got_b = across(part), other_val(part), other_both(part)
    pair = jnp.concatenate([part + got_v, got_x + got_b], axis=0)
    pair, got_line = lax.optimization_barrier((pair, got_line))
    got_across = across(got_line)
    mine = line(pair)
    weights = plan(mine, core(mine), clips)
    keep = [keep_line, core(keep_line), keep_across, core(keep_across)]
    got = [got_line, core(got_line), got_across, core(got_across)]
    out = finish(times, weights, lat, embed, keep, got)
    return out.reshape(clips, FRAME, embed.shape[1])


def warp_and_gather(latents, noise, offsets, times, embed):
    clips = latents.shape[0]
    warped = warp_noise(noise, offsets)
    panel = lax.all_gather(warped, "clip", axis=0, tiled=True)
    gram = lax.dot_general(latents, panel, NT, preferred_element_type=F32)
    square = jnp.sum(jnp.square(panel.astype(F32)), axis=1)
    part = lax.psum(square[None, :] - 2.0 * gram, "val")
    full = lax.all_gather(part, "clip", axis=0, tiled=True) * (-SCALE)
    weights = sinkhorn(full, part * (-SCALE)).astype(BF16)
    coupled = jnp.dot(weights, panel, preferred_element_type=F32)
    t = times[:, None]
    mixed = ((1.0 - t) * latents.astype(F32) + t * coupled).astype(BF16)
    cube = mixed.reshape(clips, latents.shape[1] // S, S)
    cube = lax.all_to_all(cube, "val", split_axis=2, concat_axis=1, tiled=True)
    return jnp.einsum("cps,pd->csd", cube, embed, preferred_element_type=F32).astype(BF16)


def solution(mesh):
    n, v = mesh.shape["clip"], mesh.shape["val"]
    body = functools.partial(on_device, n) if (n, v) == (16, 2) else warp_and_gather
    placed = (P("clip", "val"), P("clip", "val"), P("clip", None, None), P("clip"), P())
    return jax.shard_map(
        body, mesh=mesh, in_specs=placed, out_specs=P("clip", "val", None), check_vma=False
    )
```

```python
import functools
import math

import jax
import jax.numpy as jnp
from jax import lax
from jax.experimental import pallas as pl
from jax.experimental.pallas import tpu as pltpu
from jax.sharding import PartitionSpec as P

P_SIZE = 64
D = 5120
FR = 2
GW = 16
GH = 4
ITERS = 4
S = 128
FRAME = GW * GH
SCALE = 2.0 / math.sqrt(P_SIZE * S)
NT = (((1,), (1,)), ((), ()))
TN = (((0,), (0,)), ((), ()))
F32 = jnp.float32
BF16 = jnp.bfloat16
HBM = pl.BlockSpec(memory_space=pltpu.HBM)
VMEM = pl.BlockSpec(memory_space=pltpu.VMEM)
SMEM = pl.BlockSpec(memory_space=pltpu.SMEM)


def params(mib=48):
    return pltpu.CompilerParams(vmem_limit_bytes=mib * 1024 * 1024)


def cost(us):
    return pl.CostEstimate(flops=0, bytes_accessed=us * 3_500_000, transcendentals=0)


def lane_sources(offsets, frame, token, clips):
    square = (clips, clips)
    eye = lax.broadcasted_iota(jnp.int32, square, 0) == lax.broadcasted_iota(jnp.int32, square, 1)

    def column(k):
        spread = jnp.where(eye, jnp.broadcast_to(offsets[k : k + 1, :], square), 0)
        return jnp.sum(spread, axis=1, keepdims=True)

    shift_y = jnp.where(frame == 0, column(0), column(2))
    shift_x = jnp.where(frame == 0, column(1), column(3))
    src_row = ((token // GW) - shift_y) & (GH - 1)
    src_col = (token - shift_x) & (GW - 1)
    return frame * FRAME + src_row * GW + src_col


def gather_lanes(tile, source):
    return jnp.take_along_axis(tile, source, axis=1, mode="promise_in_bounds")


def warp_kernel(offsets, noise, out):
    clips, values = noise.shape
    lane = lax.broadcasted_iota(jnp.int32, (clips, S), 1)
    source = lane_sources(offsets, lane // FRAME, lane % FRAME, clips)
    for p in range(values // S):
        cut = slice(p * S, (p + 1) * S)
        out[:, cut] = gather_lanes(noise[:, cut].astype(F32), source).astype(BF16)


def flat_offsets(offsets):
    return offsets.transpose(1, 2, 0).reshape(FR * 2, offsets.shape[0])


def warp_noise(noise, offsets):
    return pl.pallas_call(
        warp_kernel,
        out_shape=jax.ShapeDtypeStruct(noise.shape, BF16),
        in_specs=[VMEM, VMEM],
        out_specs=VMEM,
        compiler_params=params(),
        name="warp",
    )(flat_offsets(offsets), noise)


def warp_frame(offsets, noise, frame, out):
    clips, values = noise.shape
    half = values // S // 2
    lane = lax.broadcasted_iota(jnp.int32, (clips, S), 1)
    low = lane < FRAME
    source = lane_sources(offsets, frame + lane * 0, lane % FRAME, clips)
    for q in range(half):
        near, far = slice(q * S, (q + 1) * S), slice((q + half) * S, (q + half + 1) * S)
        a, b = noise[:, near].astype(F32), noise[:, far].astype(F32)
        out[:, near] = jnp.where(low, gather_lanes(a, source), gather_lanes(b, source)).astype(BF16)


def take_frame(latents, frame, out):
    clips, values = latents.shape
    half = values // S // 2
    low = lax.broadcasted_iota(jnp.int32, (clips, S), 1) < FRAME
    for q in range(half):
        near, far = slice(q * S, (q + 1) * S), slice((q + half) * S, (q + half + 1) * S)
        a, b = latents[:, near].astype(F32), latents[:, far].astype(F32)
        first = jnp.where(low, a, pltpu.roll(b, FRAME, 1))
        second = jnp.where(low, pltpu.roll(a, FRAME, 1), b)
        out[:, near] = jnp.where(frame == 0, first, second).astype(BF16)


def split_kernel(
    offsets_in, noise_in, latents_in, keep, send, offsets, noise, latents, sems
):
    copies = [
        pltpu.make_async_copy(src, dst, sems.at[k])
        for k, (src, dst) in enumerate(
            ((offsets_in, offsets), (noise_in, noise), (latents_in, latents))
        )
    ]
    for c in copies:
        c.start()
    val = lax.axis_index("val")
    copies[0].wait()
    copies[1].wait()
    clips = noise.shape[0]
    warp_frame(offsets, noise, val, keep.at[:clips])
    warp_frame(offsets, noise, 1 - val, send.at[:clips])
    copies[2].wait()
    take_frame(latents, val, keep.at[clips:])
    take_frame(latents, 1 - val, send.at[clips:])


def in_hbm(x):
    return pltpu.with_memory_space_constraint(x, pltpu.HBM)


def split_frames(noise, latents, offsets):
    clips, values = noise.shape
    inputs = [flat_offsets(offsets), noise, latents]
    half = jax.ShapeDtypeStruct((2 * clips, values // 2), BF16)
    return pl.pallas_call(
        split_kernel,
        out_shape=[half] * 2,
        in_specs=[HBM] * 3,
        out_specs=[VMEM] * 2,
        scratch_shapes=[pltpu.VMEM(x.shape, x.dtype) for x in inputs]
        + [pltpu.SemaphoreType.DMA((3,))],
        compiler_params=params(),
        name="split",
    )(*map(in_hbm, inputs))


def stage_kernel(times, embed, table, column, sem):
    load = pltpu.make_async_copy(embed, table, sem)
    load.start()
    clips, lanes = column.shape
    row = lax.broadcasted_iota(jnp.int32, (clips, lanes), 0)
    t = jnp.zeros((clips, lanes), F32)
    for i in range(clips):
        t = jnp.where(row == i, times[i], t)
    column[...] = t
    load.wait()


def stage(times, embed):
    return pl.pallas_call(
        stage_kernel,
        out_shape=[
            jax.ShapeDtypeStruct(embed.shape, BF16),
            jax.ShapeDtypeStruct((times.shape[0], 128), F32),
        ],
        in_specs=[SMEM, HBM],
        out_specs=[VMEM] * 2,
        scratch_shapes=[pltpu.SemaphoreType.DMA],
        compiler_params=params(),
        cost_estimate=cost(2),
        name="stage",
    )(times, in_hbm(embed))


def swap_groups(x, a, clips):
    lane = lax.broadcasted_iota(jnp.int32, x.shape, 1)
    for bit in (1, 2):
        w = bit * clips
        moved = jnp.where(lane & w == 0, pltpu.roll(x, x.shape[1] - w, 1), pltpu.roll(x, w, 1))
        x = jnp.where(a & bit == 0, x, moved)
    return x


def gram_kernel(clips, lat, lat_far, lat_core, *refs):
    place = lax.axis_index("clip")
    a, x, c = place // 4, (place // 2) % 2, place % 2
    rows = 4 * clips
    out = refs[-1]
    noi = jnp.concatenate([r[...] for r in refs[:-1]], axis=0)
    cols = noi.shape[0]
    left = jnp.concatenate([lat[...], lat_far[...], lat_core[...], noi], axis=0)
    prod = lax.dot_general(left, noi, NT, preferred_element_type=F32)
    square = (cols, cols)
    eye = lax.broadcasted_iota(jnp.int32, square, 0) == lax.broadcasted_iota(jnp.int32, square, 1)
    norm = jnp.sum(jnp.where(eye, prod[rows:], 0.0), axis=0, keepdims=True)
    part = norm - 2.0 * prod[:rows]
    blocks = [part[k * clips : (k + 1) * clips] for k in range(4)]
    near0 = jnp.where(c == 0, blocks[0], blocks[2])
    near1 = jnp.where(c == 0, blocks[2], blocks[0])
    far0 = jnp.where(c == 0, blocks[1], blocks[3])
    far1 = jnp.where(c == 0, blocks[3], blocks[1])
    near = jnp.concatenate([near0, near1], axis=0)
    far = jnp.concatenate([far0, far1], axis=0)
    packed = jnp.concatenate([jnp.where(x == 0, near, far), jnp.where(x == 0, far, near)], axis=1)
    out[...] = swap_groups(packed, a, clips)


def gram_block(clips, *args):
    return pl.pallas_call(
        functools.partial(gram_kernel, clips),
        out_shape=jax.ShapeDtypeStruct((2 * clips, 128), F32),
        in_specs=[VMEM] * len(args),
        out_specs=VMEM,
        compiler_params=params(),
        cost_estimate=cost(5),
        name="gram",
    )(*args)


def sinkhorn(kernel, own):
    col = jnp.zeros((1, kernel.shape[1]), F32)
    for _ in range(ITERS):
        u = kernel + col
        top = jnp.max(u, axis=1, keepdims=True)
        row = -(top + jnp.log(jnp.sum(jnp.exp(u - top), axis=1, keepdims=True)))
        u = kernel + row
        top = jnp.max(u, axis=0, keepdims=True)
        col = -(top + jnp.log(jnp.sum(jnp.exp(u - top), axis=0, keepdims=True)))
    u = own + col
    top = jnp.max(u, axis=1, keepdims=True)
    e = jnp.exp(u - top)
    return e / jnp.sum(e, axis=1, keepdims=True)


def plan_kernel(clips, mine, other, out, full):
    place = lax.axis_index("clip")
    a, b = place // 4, place % 4
    half = 2 * clips
    low = lax.broadcasted_iota(jnp.int32, (half, 128), 1) < 64
    for s in range(mine.shape[0] // (2 * half)):
        for x in range(2):
            r = s * 2 * half
            g = mine[r + x * half : r + (x + 1) * half, :] * (-SCALE)
            h = other[r + x * half : r + (x + 1) * half, :] * (-SCALE)
            lanes = slice(x * 128, (x + 1) * 128)
            full[r : r + half, lanes] = jnp.where(low, g, pltpu.roll(h, 64, 1))
            full[r + half : r + 2 * half, lanes] = jnp.where(low, pltpu.roll(g, 64, 1), h)
    own = full[pl.ds(pl.multiple_of(b * clips, clips), clips), :]
    weights = sinkhorn(full[...], own)
    for x in range(2):
        lanes = slice(x * 128, (x + 1) * 128)
        out[:, lanes] = swap_groups(weights[:, lanes], a, clips).astype(BF16)


def plan(mine, other, clips):
    n = mine.shape[0]
    return pl.pallas_call(
        functools.partial(plan_kernel, clips),
        out_shape=jax.ShapeDtypeStruct((clips, n), BF16),
        in_specs=[VMEM] * 2,
        out_specs=VMEM,
        scratch_shapes=[pltpu.VMEM((n, n), F32)],
        compiler_params=params(),
        name="plan",
    )(mine, other)


def finish_kernel(clips, block, column, weights, lat, table, *refs):
    parts = refs[:-5]
    out, cube, lhs, result, sems = refs[-5:]
    val = lax.axis_index("val")
    t = column[:, :1]
    w = weights[...]
    values = lat.shape[1]
    step = 256
    for at in range(0, values, step):
        panel = jnp.concatenate([p[:, at : at + step] for p in parts], axis=0)
        coupled = jnp.dot(w, panel, preferred_element_type=F32)
        mixed = (1.0 - t) * lat[:, at : at + step].astype(F32) + t * coupled
        for q in range(step // S):
            cube[:, at // S + q, :] = mixed[:, q * S : (q + 1) * S]
    tiles = values // S
    half = tiles // 2
    low = lax.broadcasted_iota(jnp.int32, (tiles, S), 1) < FRAME
    for i in range(0, clips, 2):
        x, y = cube[i], cube[i + 1]
        near = jnp.where(low, x, pltpu.roll(y, FRAME, 1))
        far = jnp.where(low, pltpu.roll(x, FRAME, 1), y)
        mine = jnp.concatenate([near[:half], far[:half]], axis=0)
        other = jnp.concatenate([near[half:], far[half:]], axis=0)
        lanes = slice(i * FRAME, (i + 2) * FRAME)
        lhs[:tiles, lanes] = jnp.where(val == 0, mine, other).astype(BF16)
        lhs[tiles:, lanes] = jnp.where(val == 0, other, mine).astype(BF16)
    tokens = lhs.shape[1]
    steps = tokens // block

    def store(k):
        at = pl.multiple_of(k * block, block)
        return pltpu.make_async_copy(result.at[k], out.at[pl.ds(at, block)], sems.at[k])

    for k in range(steps):
        result[k] = lax.dot_general(
            lhs[:, k * block : (k + 1) * block], table[...], TN, preferred_element_type=F32
        ).astype(BF16)
        store(k).start()
    for k in range(steps):
        store(k).wait()


def finish(column, weights, lat, table, parts, block=128):
    clips, values = lat.shape
    tokens, width = clips * FRAME, table.shape[1]
    return pl.pallas_call(
        functools.partial(finish_kernel, clips, block),
        out_shape=jax.ShapeDtypeStruct((tokens, width), BF16),
        in_specs=[VMEM] * (4 + len(parts)),
        out_specs=HBM,
        scratch_shapes=[
            pltpu.VMEM((clips, values // S, S), F32),
            pltpu.VMEM((P_SIZE, tokens), BF16),
            pltpu.VMEM((tokens // block, block, width), BF16),
            pltpu.SemaphoreType.DMA((tokens // block,)),
        ],
        compiler_params=params(),
        name="finish",
    )(column, weights, lat, table, *parts)


def flip(n, bit):
    return [(i, i ^ bit) for i in range(n)]


def on_device(n, latents, noise, offsets, times, embed):
    clips = latents.shape[0]

    def core(x):
        return lax.ppermute(x, "clip", flip(n, 1))

    def across(x):
        return lax.ppermute(x, "clip", flip(n, 2))

    def along(x, k):
        return lax.ppermute(x, "clip", flip(n, 4 * k))

    def other_val(x):
        return lax.ppermute(x, "val", [(0, 1), (1, 0)])

    def other_both(x):
        pairs = [(2 * i + v, 2 * (i ^ 2) + 1 - v) for i in range(n) for v in range(2)]
        return lax.ppermute(x, ("clip", "val"), pairs)

    def beside(*x):
        return jnp.concatenate(x, axis=1)

    def below(*x):
        return jnp.concatenate(x, axis=0)

    keep, send = split_frames(noise, latents, offsets)
    got, keep_far = lax.optimization_barrier((other_val(send), across(keep)))
    own, far_own = beside(keep, got), beside(keep_far, across(got))
    lat, lat_far = own[clips:], far_own[clips:]
    noi = [own[:clips]]
    noi.append(along(noi[0], 1))
    noi.append(along(noi[0], 2))
    noi.append(along(noi[2], 1))
    lat_core = core(below(lat, lat_far))
    times, embed, _ = lax.optimization_barrier((times, embed, keep))
    table, column = stage(times, embed)
    lat_core, table, column = lax.optimization_barrier((lat_core, table, column))
    part = gram_block(clips, lat, lat_far, lat_core, *noi)
    got_x, got_v, got_b = across(part), other_val(part), other_both(part)
    far_mid, got_x = lax.optimization_barrier((across(below(noi[1], noi[2])), got_x))
    last, got_x = lax.optimization_barrier((noi[3], got_x))
    pair = below(part + got_v, got_x + got_b)
    far_last, *rows = lax.optimization_barrier([across(last)] + [along(pair, k) for k in (1, 2, 3)])
    mine = below(pair, *rows)
    weights = plan(mine, core(mine), clips)
    far = [far_own[:clips], far_mid]
    parts = [*noi, core(below(*noi)), *far, far_last, core(below(*far)), core(far_last)]
    out = finish(column, weights, lat, table, parts)
    return out.reshape(clips, FRAME, out.shape[1])


def warp_and_gather(latents, noise, offsets, times, embed):
    clips = latents.shape[0]
    warped = warp_noise(noise, offsets)
    panel = lax.all_gather(warped, "clip", axis=0, tiled=True)
    gram = lax.dot_general(latents, panel, NT, preferred_element_type=F32)
    square = jnp.sum(jnp.square(panel.astype(F32)), axis=1)
    part = lax.psum(square[None, :] - 2.0 * gram, "val")
    full = lax.all_gather(part, "clip", axis=0, tiled=True) * (-SCALE)
    weights = sinkhorn(full, part * (-SCALE)).astype(BF16)
    coupled = jnp.dot(weights, panel, preferred_element_type=F32)
    t = times[:, None]
    mixed = ((1.0 - t) * latents.astype(F32) + t * coupled).astype(BF16)
    cube = mixed.reshape(clips, latents.shape[1] // S, S)
    cube = lax.all_to_all(cube, "val", split_axis=2, concat_axis=1, tiled=True)
    return jnp.einsum("cps,pd->csd", cube, embed, preferred_element_type=F32).astype(BF16)


def solution(mesh):
    n, v = mesh.shape["clip"], mesh.shape["val"]
    body = functools.partial(on_device, n) if (n, v) == (16, 2) else warp_and_gather
    placed = (P("clip", "val"), P("clip", "val"), P("clip", None, None), P("clip"), P())
    return jax.shard_map(
        body, mesh=mesh, in_specs=placed, out_specs=P("clip", "val", None), check_vma=False
    )
```

```python
import functools
import math

import jax
import jax.numpy as jnp
from jax import lax
from jax.experimental import pallas as pl
from jax.experimental.pallas import tpu as pltpu
from jax.sharding import PartitionSpec as P

P_SIZE = 64
D = 5120
FR = 2
GW = 16
GH = 4
ITERS = 4
S = 128
FRAME = GW * GH
SCALE = 2.0 / math.sqrt(P_SIZE * S)
NT = (((1,), (1,)), ((), ()))
TN = (((0,), (0,)), ((), ()))
F32 = jnp.float32
BF16 = jnp.bfloat16
HBM = pl.BlockSpec(memory_space=pltpu.HBM)
VMEM = pl.BlockSpec(memory_space=pltpu.VMEM)
SMEM = pl.BlockSpec(memory_space=pltpu.SMEM)


def params(mib=48):
    return pltpu.CompilerParams(vmem_limit_bytes=mib * 1024 * 1024)


def cost(us):
    return pl.CostEstimate(flops=0, bytes_accessed=us * 3_500_000, transcendentals=0)


def lane_sources(offsets, frame, token, clips):
    square = (clips, clips)
    eye = lax.broadcasted_iota(jnp.int32, square, 0) == lax.broadcasted_iota(jnp.int32, square, 1)

    def column(k):
        spread = jnp.where(eye, jnp.broadcast_to(offsets[k : k + 1, :], square), 0)
        return jnp.sum(spread, axis=1, keepdims=True)

    shift_y = jnp.where(frame == 0, column(0), column(2))
    shift_x = jnp.where(frame == 0, column(1), column(3))
    src_row = ((token // GW) - shift_y) & (GH - 1)
    src_col = (token - shift_x) & (GW - 1)
    return frame * FRAME + src_row * GW + src_col


def gather_lanes(tile, source):
    return jnp.take_along_axis(tile, source, axis=1, mode="promise_in_bounds")


def warp_kernel(offsets, noise, out):
    clips, values = noise.shape
    lane = lax.broadcasted_iota(jnp.int32, (clips, S), 1)
    source = lane_sources(offsets, lane // FRAME, lane % FRAME, clips)
    for p in range(values // S):
        cut = slice(p * S, (p + 1) * S)
        out[:, cut] = gather_lanes(noise[:, cut].astype(F32), source).astype(BF16)


def flat_offsets(offsets):
    return offsets.transpose(1, 2, 0).reshape(FR * 2, offsets.shape[0])


def warp_noise(noise, offsets):
    return pl.pallas_call(
        warp_kernel,
        out_shape=jax.ShapeDtypeStruct(noise.shape, BF16),
        in_specs=[VMEM, VMEM],
        out_specs=VMEM,
        compiler_params=params(),
        name="warp",
    )(flat_offsets(offsets), noise)


def warp_frame(offsets, noise, frame, out):
    clips, values = noise.shape
    half = values // S // 2
    lane = lax.broadcasted_iota(jnp.int32, (clips, S), 1)
    low = lane < FRAME
    source = lane_sources(offsets, frame + lane * 0, lane % FRAME, clips)
    for q in range(half):
        near, far = slice(q * S, (q + 1) * S), slice((q + half) * S, (q + half + 1) * S)
        a, b = noise[:, near].astype(F32), noise[:, far].astype(F32)
        out[:, near] = jnp.where(low, gather_lanes(a, source), gather_lanes(b, source)).astype(BF16)


def take_frame(latents, frame, out):
    clips, values = latents.shape
    half = values // S // 2
    low = lax.broadcasted_iota(jnp.int32, (clips, S), 1) < FRAME
    for q in range(half):
        near, far = slice(q * S, (q + 1) * S), slice((q + half) * S, (q + half + 1) * S)
        a, b = latents[:, near].astype(F32), latents[:, far].astype(F32)
        first = jnp.where(low, a, pltpu.roll(b, FRAME, 1))
        second = jnp.where(low, pltpu.roll(a, FRAME, 1), b)
        out[:, near] = jnp.where(frame == 0, first, second).astype(BF16)


def split_kernel(
    offsets_in, noise_in, latents_in, noise_out, lat_out, offsets, noise, latents, sems
):
    copies = [
        pltpu.make_async_copy(src, dst, sems.at[k])
        for k, (src, dst) in enumerate(
            ((offsets_in, offsets), (noise_in, noise), (latents_in, latents))
        )
    ]
    for c in copies:
        c.start()
    val = lax.axis_index("val")
    copies[0].wait()
    copies[1].wait()
    cut = noise.shape[1] // 2
    warp_frame(offsets, noise, val, noise_out.at[:, :cut])
    warp_frame(offsets, noise, 1 - val, noise_out.at[:, cut:])
    copies[2].wait()
    take_frame(latents, val, lat_out.at[:, :cut])
    take_frame(latents, 1 - val, lat_out.at[:, cut:])


def in_hbm(x):
    return pltpu.with_memory_space_constraint(x, pltpu.HBM)


def split_frames(noise, latents, offsets):
    inputs = [flat_offsets(offsets), noise, latents]
    return pl.pallas_call(
        split_kernel,
        out_shape=[jax.ShapeDtypeStruct(noise.shape, BF16)] * 2,
        in_specs=[HBM] * 3,
        out_specs=[VMEM] * 2,
        scratch_shapes=[pltpu.VMEM(x.shape, x.dtype) for x in inputs]
        + [pltpu.SemaphoreType.DMA((3,))],
        compiler_params=params(),
        name="split",
    )(*map(in_hbm, inputs))


def stage_kernel(times_in, embed, table, column, times, sems):
    load = pltpu.make_async_copy(embed, table, sems.at[0])
    load.start()
    small = pltpu.make_async_copy(times_in, times, sems.at[1])
    small.start()
    clips, lanes = column.shape
    row = lax.broadcasted_iota(jnp.int32, (clips, lanes), 0)
    t = jnp.zeros((clips, lanes), F32)
    small.wait()
    for i in range(clips):
        t = jnp.where(row == i, times[i], t)
    column[...] = t
    load.wait()


def stage(times, embed):
    return pl.pallas_call(
        stage_kernel,
        out_shape=[
            jax.ShapeDtypeStruct(embed.shape, BF16),
            jax.ShapeDtypeStruct((times.shape[0], 128), F32),
        ],
        in_specs=[HBM] * 2,
        out_specs=[VMEM] * 2,
        scratch_shapes=[pltpu.SMEM(times.shape, F32), pltpu.SemaphoreType.DMA((2,))],
        compiler_params=params(),
        cost_estimate=cost(2),
        name="stage",
    )(in_hbm(times), in_hbm(embed))


def swap_groups(x, a, clips):
    lane = lax.broadcasted_iota(jnp.int32, x.shape, 1)
    for bit in (1, 2):
        w = bit * clips
        moved = jnp.where(lane & w == 0, pltpu.roll(x, x.shape[1] - w, 1), pltpu.roll(x, w, 1))
        x = jnp.where(a & bit == 0, x, moved)
    return x


def gram_kernel(clips, lat, lat_far, lat_core, *refs):
    place = lax.axis_index("clip")
    a, x, c = place // 4, (place // 2) % 2, place % 2
    rows = 4 * clips
    out = refs[-1]
    noi = jnp.concatenate([r[...] for r in refs[:-1]], axis=0)
    cols = noi.shape[0]
    left = jnp.concatenate([lat[...], lat_far[...], lat_core[...], noi], axis=0)
    prod = lax.dot_general(left, noi, NT, preferred_element_type=F32)
    square = (cols, cols)
    eye = lax.broadcasted_iota(jnp.int32, square, 0) == lax.broadcasted_iota(jnp.int32, square, 1)
    norm = jnp.sum(jnp.where(eye, prod[rows:], 0.0), axis=0, keepdims=True)
    part = norm - 2.0 * prod[:rows]
    blocks = [part[k * clips : (k + 1) * clips] for k in range(4)]
    near0 = jnp.where(c == 0, blocks[0], blocks[2])
    near1 = jnp.where(c == 0, blocks[2], blocks[0])
    far0 = jnp.where(c == 0, blocks[1], blocks[3])
    far1 = jnp.where(c == 0, blocks[3], blocks[1])
    near = jnp.concatenate([near0, near1], axis=0)
    far = jnp.concatenate([far0, far1], axis=0)
    packed = jnp.concatenate([jnp.where(x == 0, near, far), jnp.where(x == 0, far, near)], axis=1)
    out[...] = swap_groups(packed, a, clips)


def gram_block(clips, *args):
    return pl.pallas_call(
        functools.partial(gram_kernel, clips),
        out_shape=jax.ShapeDtypeStruct((2 * clips, 128), F32),
        in_specs=[VMEM] * len(args),
        out_specs=VMEM,
        compiler_params=params(),
        cost_estimate=cost(5),
        name="gram",
    )(*args)


def sinkhorn(kernel, own):
    col = jnp.zeros((1, kernel.shape[1]), F32)
    for _ in range(ITERS):
        u = kernel + col
        top = jnp.max(u, axis=1, keepdims=True)
        row = -(top + jnp.log(jnp.sum(jnp.exp(u - top), axis=1, keepdims=True)))
        u = kernel + row
        top = jnp.max(u, axis=0, keepdims=True)
        col = -(top + jnp.log(jnp.sum(jnp.exp(u - top), axis=0, keepdims=True)))
    u = own + col
    top = jnp.max(u, axis=1, keepdims=True)
    e = jnp.exp(u - top)
    return e / jnp.sum(e, axis=1, keepdims=True)


def plan_kernel(clips, mine, other, out, full):
    place = lax.axis_index("clip")
    a, b = place // 4, place % 4
    half = 2 * clips
    low = lax.broadcasted_iota(jnp.int32, (half, 128), 1) < 64
    for s in range(mine.shape[0] // (2 * half)):
        for x in range(2):
            r = s * 2 * half
            g = mine[r + x * half : r + (x + 1) * half, :] * (-SCALE)
            h = other[r + x * half : r + (x + 1) * half, :] * (-SCALE)
            lanes = slice(x * 128, (x + 1) * 128)
            full[r : r + half, lanes] = jnp.where(low, g, pltpu.roll(h, 64, 1))
            full[r + half : r + 2 * half, lanes] = jnp.where(low, pltpu.roll(g, 64, 1), h)
    own = full[pl.ds(pl.multiple_of(b * clips, clips), clips), :]
    weights = sinkhorn(full[...], own)
    for x in range(2):
        lanes = slice(x * 128, (x + 1) * 128)
        out[:, lanes] = swap_groups(weights[:, lanes], a, clips).astype(BF16)


def plan(mine, other, clips):
    n = mine.shape[0]
    return pl.pallas_call(
        functools.partial(plan_kernel, clips),
        out_shape=jax.ShapeDtypeStruct((clips, n), BF16),
        in_specs=[VMEM] * 2,
        out_specs=VMEM,
        scratch_shapes=[pltpu.VMEM((n, n), F32)],
        compiler_params=params(),
        name="plan",
    )(mine, other)


def finish_kernel(clips, block, layout, column, weights, lat_keep, lat_got, table, *refs):
    parts = refs[:-5]
    out, cube, lhs, result, sems = refs[-5:]
    val = lax.axis_index("val")
    t = column[:, :1]
    w = weights[...]
    cut = lat_got.shape[1]
    step = 256
    for h, lat in enumerate((lat_keep, lat_got)):
        for at in range(0, cut, step):
            lanes = slice(at, at + step)
            panel = jnp.concatenate([parts[k][r : r + clips, lanes] for k, r in layout[h]], axis=0)
            coupled = jnp.dot(w, panel, preferred_element_type=F32)
            mixed = (1.0 - t) * lat[:, lanes].astype(F32) + t * coupled
            for q in range(step // S):
                cube[:, (h * cut + at) // S + q, :] = mixed[:, q * S : (q + 1) * S]
    values = 2 * cut
    tiles = values // S
    half = tiles // 2
    low = lax.broadcasted_iota(jnp.int32, (tiles, S), 1) < FRAME
    for i in range(0, clips, 2):
        x, y = cube[i], cube[i + 1]
        near = jnp.where(low, x, pltpu.roll(y, FRAME, 1))
        far = jnp.where(low, pltpu.roll(x, FRAME, 1), y)
        mine = jnp.concatenate([near[:half], far[:half]], axis=0)
        other = jnp.concatenate([near[half:], far[half:]], axis=0)
        lanes = slice(i * FRAME, (i + 2) * FRAME)
        lhs[:tiles, lanes] = jnp.where(val == 0, mine, other).astype(BF16)
        lhs[tiles:, lanes] = jnp.where(val == 0, other, mine).astype(BF16)
    tokens = lhs.shape[1]
    steps = tokens // block

    def store(k):
        at = pl.multiple_of(k * block, block)
        return pltpu.make_async_copy(result.at[k], out.at[pl.ds(at, block)], sems.at[k])

    for k in range(steps):
        result[k] = lax.dot_general(
            lhs[:, k * block : (k + 1) * block], table[...], TN, preferred_element_type=F32
        ).astype(BF16)
        store(k).start()
    for k in range(steps):
        store(k).wait()


def finish(column, weights, lat_keep, lat_got, table, parts, layout, block=128):
    clips, values = lat_keep.shape
    tokens, width = clips * FRAME, table.shape[1]
    return pl.pallas_call(
        functools.partial(finish_kernel, clips, block, layout),
        out_shape=jax.ShapeDtypeStruct((tokens, width), BF16),
        in_specs=[VMEM] * (5 + len(parts)),
        out_specs=HBM,
        scratch_shapes=[
            pltpu.VMEM((clips, values // S, S), F32),
            pltpu.VMEM((P_SIZE, tokens), BF16),
            pltpu.VMEM((tokens // block, block, width), BF16),
            pltpu.SemaphoreType.DMA((tokens // block,)),
        ],
        compiler_params=params(),
        name="finish",
    )(column, weights, lat_keep, lat_got, table, *parts)


def stack_kernel(*refs):
    parts, (firsts, seconds) = refs[:-2], refs[-2:]
    clips, values = parts[0].shape
    cut = values // 2
    for k, part in enumerate(parts):
        firsts[k * clips : (k + 1) * clips, :] = part[:, :cut]
        if k:
            seconds[(k - 1) * clips : k * clips, :] = part[:, cut:]


def stack(parts):
    clips, values = parts[0].shape
    shapes = [(k * clips, values // 2) for k in (len(parts), len(parts) - 1)]
    return pl.pallas_call(
        stack_kernel,
        out_shape=[jax.ShapeDtypeStruct(x, BF16) for x in shapes],
        in_specs=[VMEM] * len(parts),
        out_specs=[VMEM] * 2,
        compiler_params=params(),
        cost_estimate=cost(3),
        name="stack",
    )(*parts)


def flip(n, bit):
    return [(i, i ^ bit) for i in range(n)]


def on_device(n, latents, noise, offsets, times, embed):
    clips = latents.shape[0]

    def core(x):
        return lax.ppermute(x, "clip", flip(n, 1))

    def across(x):
        return lax.ppermute(x, "clip", flip(n, 2))

    def along(x, k):
        return lax.ppermute(x, "clip", flip(n, 4 * k))

    def other_val(x):
        return lax.ppermute(x, "val", [(0, 1), (1, 0)])

    def other_both(x):
        pairs = [(2 * i + v, 2 * (i ^ 2) + 1 - v) for i in range(n) for v in range(2)]
        return lax.ppermute(x, ("clip", "val"), pairs)

    def beside(*x):
        return jnp.concatenate(x, axis=1)

    def below(*x):
        return jnp.concatenate(x, axis=0)

    own, lat = split_frames(noise, latents, offsets)
    cut = own.shape[1] // 2
    noi = [own]
    noi.append(along(own, 1))
    noi.append(along(own, 2))
    noi.append(along(noi[2], 1))
    keep = [x[:, :cut] for x in noi]
    send = [x[:, cut:] for x in noi]
    times, embed, _ = lax.optimization_barrier((times, embed, own))
    table, column = stage(times, embed)
    lat_late, own_late, table, column = lax.optimization_barrier((lat, own, table, column))
    got_own = other_val(below(own_late[:, cut:], lat_late[:, cut:]))
    lat_far, _ = lax.optimization_barrier((across(lat_late), noi[2]))
    lat_core = core(below(lat, lat_far))
    part = gram_block(clips, lat, lat_far, lat_core, *noi)
    got_x, got_v, got_b = across(part), other_val(part), other_both(part)
    own_late, _ = lax.optimization_barrier((own, lat_far))
    to_far, to_val = stack([own_late, *noi[1:3]])
    got_mid, far = other_val(to_val), across(to_far)
    got_last = other_val(send[3])
    got_own, got_mid, far, got_x = lax.optimization_barrier((got_own, got_mid, far, got_x))
    got, lat_got = below(got_own[:clips], got_mid, got_last), got_own[clips:]
    far_rest = across(below(keep[3], got))
    pair = below(part + got_v, got_x + got_b)
    rows = [along(pair, k) for k in (1, 2, 3)]
    far_rest, *rows = lax.optimization_barrier([far_rest] + rows)
    mine = below(pair, *rows)
    line = below(*keep)
    beside_core = [core(x) for x in (line, got, far)]
    other, *beside_core = lax.optimization_barrier([core(mine)] + beside_core)
    weights = plan(mine, other, clips)
    parts = [line, beside_core[0], got, beside_core[1]]
    parts += [far, beside_core[2], far_rest, core(far_rest)]
    first, second = [], []
    for k in (0, 1):
        first += [(k, s * clips) for s in range(4)]
        second += [(2 + k, s * clips) for s in range(4)]
    for k in (0, 1):
        first += [(4 + k, s * clips) for s in range(3)] + [(6 + k, 0)]
        second += [(6 + k, s * clips) for s in range(1, 5)]
    out = finish(column, weights, lat, lat_got, table, parts, (first, second))
    return out.reshape(clips, FRAME, out.shape[1])


def warp_and_gather(latents, noise, offsets, times, embed):
    clips = latents.shape[0]
    warped = warp_noise(noise, offsets)
    panel = lax.all_gather(warped, "clip", axis=0, tiled=True)
    gram = lax.dot_general(latents, panel, NT, preferred_element_type=F32)
    square = jnp.sum(jnp.square(panel.astype(F32)), axis=1)
    part = lax.psum(square[None, :] - 2.0 * gram, "val")
    full = lax.all_gather(part, "clip", axis=0, tiled=True) * (-SCALE)
    weights = sinkhorn(full, part * (-SCALE)).astype(BF16)
    coupled = jnp.dot(weights, panel, preferred_element_type=F32)
    t = times[:, None]
    mixed = ((1.0 - t) * latents.astype(F32) + t * coupled).astype(BF16)
    cube = mixed.reshape(clips, latents.shape[1] // S, S)
    cube = lax.all_to_all(cube, "val", split_axis=2, concat_axis=1, tiled=True)
    return jnp.einsum("cps,pd->csd", cube, embed, preferred_element_type=F32).astype(BF16)


def solution(mesh):
    n, v = mesh.shape["clip"], mesh.shape["val"]
    body = functools.partial(on_device, n) if (n, v) == (16, 2) else warp_and_gather
    placed = (P("clip", "val"), P("clip", "val"), P("clip", None, None), P("clip"), P())
    return jax.shard_map(
        body, mesh=mesh, in_specs=placed, out_specs=P("clip", "val", None), check_vma=False
    )
```

```python
import functools
import math

import jax
import jax.numpy as jnp
from jax import lax
from jax.experimental import pallas as pl
from jax.experimental.pallas import tpu as pltpu
from jax.sharding import PartitionSpec as P

P_SIZE = 64
D = 5120
FR = 2
GW = 16
GH = 4
ITERS = 4
S = 128
FRAME = GW * GH
SCALE = 2.0 / math.sqrt(P_SIZE * S)
NT = (((1,), (1,)), ((), ()))
TN = (((0,), (0,)), ((), ()))
F32 = jnp.float32
BF16 = jnp.bfloat16
HBM = pl.BlockSpec(memory_space=pltpu.HBM)
VMEM = pl.BlockSpec(memory_space=pltpu.VMEM)
SMEM = pl.BlockSpec(memory_space=pltpu.SMEM)


def params(mib=48):
    return pltpu.CompilerParams(vmem_limit_bytes=mib * 1024 * 1024)


def cost(us):
    return pl.CostEstimate(flops=0, bytes_accessed=us * 3_500_000, transcendentals=0)


def lane_sources(offsets, frame, token, clips):
    square = (clips, clips)
    eye = lax.broadcasted_iota(jnp.int32, square, 0) == lax.broadcasted_iota(jnp.int32, square, 1)

    def column(k):
        spread = jnp.where(eye, jnp.broadcast_to(offsets[k : k + 1, :], square), 0)
        return jnp.sum(spread, axis=1, keepdims=True)

    shift_y = jnp.where(frame == 0, column(0), column(2))
    shift_x = jnp.where(frame == 0, column(1), column(3))
    src_row = ((token // GW) - shift_y) & (GH - 1)
    src_col = (token - shift_x) & (GW - 1)
    return frame * FRAME + src_row * GW + src_col


def gather_lanes(tile, source):
    return jnp.take_along_axis(tile, source, axis=1, mode="promise_in_bounds")


def warp_kernel(offsets, noise, out):
    clips, values = noise.shape
    lane = lax.broadcasted_iota(jnp.int32, (clips, S), 1)
    source = lane_sources(offsets, lane // FRAME, lane % FRAME, clips)
    for p in range(values // S):
        cut = slice(p * S, (p + 1) * S)
        out[:, cut] = gather_lanes(noise[:, cut].astype(F32), source).astype(BF16)


def flat_offsets(offsets):
    return offsets.transpose(1, 2, 0).reshape(FR * 2, offsets.shape[0])


def warp_noise(noise, offsets):
    return pl.pallas_call(
        warp_kernel,
        out_shape=jax.ShapeDtypeStruct(noise.shape, BF16),
        in_specs=[VMEM, VMEM],
        out_specs=VMEM,
        compiler_params=params(),
        name="warp",
    )(flat_offsets(offsets), noise)


def warp_frame(offsets, noise, frame, out):
    clips, values = noise.shape
    half = values // S // 2
    lane = lax.broadcasted_iota(jnp.int32, (clips, S), 1)
    low = lane < FRAME
    source = lane_sources(offsets, frame + lane * 0, lane % FRAME, clips)
    for q in range(half):
        near, far = slice(q * S, (q + 1) * S), slice((q + half) * S, (q + half + 1) * S)
        a, b = noise[:, near].astype(F32), noise[:, far].astype(F32)
        out[:, near] = jnp.where(low, gather_lanes(a, source), gather_lanes(b, source)).astype(BF16)


def take_frame(latents, frame, out):
    clips, values = latents.shape
    half = values // S // 2
    low = lax.broadcasted_iota(jnp.int32, (clips, S), 1) < FRAME
    for q in range(half):
        near, far = slice(q * S, (q + 1) * S), slice((q + half) * S, (q + half + 1) * S)
        a, b = latents[:, near].astype(F32), latents[:, far].astype(F32)
        first = jnp.where(low, a, pltpu.roll(b, FRAME, 1))
        second = jnp.where(low, pltpu.roll(a, FRAME, 1), b)
        out[:, near] = jnp.where(frame == 0, first, second).astype(BF16)


def split_kernel(offsets_in, noise_in, noise_out, offsets, noise, sems):
    small = pltpu.make_async_copy(offsets_in, offsets, sems.at[0])
    load = pltpu.make_async_copy(noise_in, noise, sems.at[1])
    small.start()
    load.start()
    val = lax.axis_index("val")
    cut = noise.shape[1] // 2
    small.wait()
    load.wait()
    warp_frame(offsets, noise, val, noise_out.at[:, :cut])
    warp_frame(offsets, noise, 1 - val, noise_out.at[:, cut:])


def in_hbm(x):
    return pltpu.with_memory_space_constraint(x, pltpu.HBM)


def split_frames(noise, offsets):
    inputs = [flat_offsets(offsets), noise]
    return pl.pallas_call(
        split_kernel,
        out_shape=jax.ShapeDtypeStruct(noise.shape, BF16),
        in_specs=[HBM] * 2,
        out_specs=VMEM,
        scratch_shapes=[pltpu.VMEM(x.shape, x.dtype) for x in inputs]
        + [pltpu.SemaphoreType.DMA((2,))],
        compiler_params=params(),
        name="split",
    )(*map(in_hbm, inputs))


def stage_kernel(times_in, embed, latents_in, table, column, lat, times, latents, sems):
    small = pltpu.make_async_copy(times_in, times, sems.at[0])
    load = pltpu.make_async_copy(latents_in, latents, sems.at[1])
    large = pltpu.make_async_copy(embed, table, sems.at[2])
    for copy in (small, load, large):
        copy.start()
    val = lax.axis_index("val")
    clips, lanes = column.shape
    row = lax.broadcasted_iota(jnp.int32, (clips, lanes), 0)
    t = jnp.zeros((clips, lanes), F32)
    small.wait()
    for i in range(clips):
        t = jnp.where(row == i, times[i], t)
    column[...] = t
    cut = latents.shape[1] // 2
    load.wait()
    take_frame(latents, val, lat.at[:, :cut])
    take_frame(latents, 1 - val, lat.at[:, cut:])
    large.wait()


def stage(times, embed, latents):
    return pl.pallas_call(
        stage_kernel,
        out_shape=[
            jax.ShapeDtypeStruct(embed.shape, BF16),
            jax.ShapeDtypeStruct((times.shape[0], 128), F32),
            jax.ShapeDtypeStruct(latents.shape, BF16),
        ],
        in_specs=[HBM] * 3,
        out_specs=[VMEM] * 3,
        scratch_shapes=[
            pltpu.SMEM(times.shape, F32),
            pltpu.VMEM(latents.shape, BF16),
            pltpu.SemaphoreType.DMA((3,)),
        ],
        compiler_params=params(),
        cost_estimate=cost(2),
        name="stage",
    )(*map(in_hbm, (times, embed, latents)))


def swap_groups(x, a, clips):
    lane = lax.broadcasted_iota(jnp.int32, x.shape, 1)
    for bit in (1, 2):
        w = bit * clips
        moved = jnp.where(lane & w == 0, pltpu.roll(x, x.shape[1] - w, 1), pltpu.roll(x, w, 1))
        x = jnp.where(a & bit == 0, x, moved)
    return x


def gram_kernel(clips, lat, lat_far, lat_core, *refs):
    place = lax.axis_index("clip")
    a, x, c = place // 4, (place // 2) % 2, place % 2
    rows = 4 * clips
    out = refs[-1]
    noi = jnp.concatenate([r[...] for r in refs[:-1]], axis=0)
    cols = noi.shape[0]
    left = jnp.concatenate([lat[...], lat_far[...], lat_core[...], noi], axis=0)
    prod = lax.dot_general(left, noi, NT, preferred_element_type=F32)
    square = (cols, cols)
    eye = lax.broadcasted_iota(jnp.int32, square, 0) == lax.broadcasted_iota(jnp.int32, square, 1)
    norm = jnp.sum(jnp.where(eye, prod[rows:], 0.0), axis=0, keepdims=True)
    part = norm - 2.0 * prod[:rows]
    blocks = [part[k * clips : (k + 1) * clips] for k in range(4)]
    near0 = jnp.where(c == 0, blocks[0], blocks[2])
    near1 = jnp.where(c == 0, blocks[2], blocks[0])
    far0 = jnp.where(c == 0, blocks[1], blocks[3])
    far1 = jnp.where(c == 0, blocks[3], blocks[1])
    near = jnp.concatenate([near0, near1], axis=0)
    far = jnp.concatenate([far0, far1], axis=0)
    packed = jnp.concatenate([jnp.where(x == 0, near, far), jnp.where(x == 0, far, near)], axis=1)
    out[...] = swap_groups(packed, a, clips)


def gram_block(clips, *args):
    return pl.pallas_call(
        functools.partial(gram_kernel, clips),
        out_shape=jax.ShapeDtypeStruct((2 * clips, 128), F32),
        in_specs=[VMEM] * len(args),
        out_specs=VMEM,
        compiler_params=params(),
        cost_estimate=cost(5),
        name="gram",
    )(*args)


def sinkhorn(kernel):
    top = jnp.max(kernel, axis=1, keepdims=True)
    row = top + jnp.log(jnp.sum(jnp.exp(kernel - top), axis=1, keepdims=True))
    u = kernel - row
    top = jnp.max(u, axis=0, keepdims=True)
    share = jnp.exp(u - top)
    right = 1.0 / jnp.sum(share, axis=0, keepdims=True)
    for _ in range(ITERS - 1):
        left = 1.0 / jnp.sum(share * right, axis=1, keepdims=True)
        right = 1.0 / jnp.sum(share * left, axis=0, keepdims=True)
    return share, right


def softmax_rows(share, right):
    e = share * right
    return e / jnp.sum(e, axis=1, keepdims=True)


def plan_kernel(clips, mine, other, out, full):
    place = lax.axis_index("clip")
    a, b = place // 4, place % 4
    half = 2 * clips
    low = lax.broadcasted_iota(jnp.int32, (half, 128), 1) < 64
    for s in range(mine.shape[0] // (2 * half)):
        for x in range(2):
            r = s * 2 * half
            g = mine[r + x * half : r + (x + 1) * half, :] * (-SCALE)
            h = other[r + x * half : r + (x + 1) * half, :] * (-SCALE)
            lanes = slice(x * 128, (x + 1) * 128)
            full[r : r + half, lanes] = jnp.where(low, g, pltpu.roll(h, 64, 1))
            full[r + half : r + 2 * half, lanes] = jnp.where(low, pltpu.roll(g, 64, 1), h)
    share, right = sinkhorn(full[...])
    full[...] = share
    own = full[pl.ds(pl.multiple_of(b * clips, clips), clips), :]
    weights = softmax_rows(own, right)
    for x in range(2):
        lanes = slice(x * 128, (x + 1) * 128)
        out[:, lanes] = swap_groups(weights[:, lanes], a, clips).astype(BF16)


def plan(mine, other, clips):
    n = mine.shape[0]
    return pl.pallas_call(
        functools.partial(plan_kernel, clips),
        out_shape=jax.ShapeDtypeStruct((clips, n), BF16),
        in_specs=[VMEM] * 2,
        out_specs=VMEM,
        scratch_shapes=[pltpu.VMEM((n, n), F32)],
        compiler_params=params(),
        name="plan",
    )(mine, other)


def finish_kernel(clips, block, layout, column, weights, lat_keep, lat_got, table, *refs):
    parts = refs[:-4]
    out, cube, result, sems = refs[-4:]
    val = lax.axis_index("val")
    t = column[:, :1]
    w = weights[...]
    cut = lat_got.shape[1]
    step = 256
    for h, lat in enumerate((lat_keep, lat_got)):
        for at in range(0, cut, step):
            lanes = slice(at, at + step)
            panel = jnp.concatenate([parts[k][r : r + clips, lanes] for k, r in layout[h]], axis=0)
            coupled = jnp.dot(w, panel, preferred_element_type=F32)
            mixed = (1.0 - t) * lat[:, lanes].astype(F32) + t * coupled
            for q in range(step // S):
                cube[:, (h * cut + at) // S + q, :] = mixed[:, q * S : (q + 1) * S]
    values = 2 * cut
    tiles = values // S
    half = tiles // 2
    low = lax.broadcasted_iota(jnp.int32, (tiles, S), 1) < FRAME
    per_pair = 2 * FRAME // block
    steps = clips * FRAME // block

    def store(k):
        return pltpu.make_async_copy(result.at[k], out.at[pl.ds(k * block, block)], sems.at[k])

    for k in range(clips // 2):
        x, y = cube[2 * k], cube[2 * k + 1]
        near = jnp.where(low, x, pltpu.roll(y, FRAME, 1))
        far = jnp.where(low, pltpu.roll(x, FRAME, 1), y)
        mine = jnp.concatenate([near[:half], far[:half]], axis=0)
        other = jnp.concatenate([near[half:], far[half:]], axis=0)
        both = [jnp.where(val == 0, mine, other), jnp.where(val == 0, other, mine)]
        lhs = jnp.concatenate(both, axis=0).astype(BF16)
        for j in range(per_pair):
            step = k * per_pair + j
            tokens = lhs[:, j * block : (j + 1) * block]
            full = lax.dot_general(tokens, table[...], TN, preferred_element_type=F32)
            result[step] = full.astype(BF16)
            store(step).start()
    for k in range(steps):
        store(k).wait()


def finish(column, weights, lat_keep, lat_got, table, parts, layout, block=FRAME):
    clips, values = lat_keep.shape
    tokens, width = clips * FRAME, table.shape[1]
    return pl.pallas_call(
        functools.partial(finish_kernel, clips, block, layout),
        out_shape=jax.ShapeDtypeStruct((tokens, width), BF16),
        in_specs=[VMEM] * (5 + len(parts)),
        out_specs=HBM,
        scratch_shapes=[
            pltpu.VMEM((clips, values // S, S), F32),
            pltpu.VMEM((tokens // block, block, width), BF16),
            pltpu.SemaphoreType.DMA((tokens // block,)),
        ],
        compiler_params=params(),
        name="finish",
    )(column, weights, lat_keep, lat_got, table, *parts)


def stack_kernel(*refs):
    parts, (firsts, seconds) = refs[:-2], refs[-2:]
    clips, values = parts[0].shape
    cut = values // 2
    for k, part in enumerate(parts):
        firsts[k * clips : (k + 1) * clips, :] = part[:, :cut]
        if k:
            seconds[(k - 1) * clips : k * clips, :] = part[:, cut:]


def stack(parts):
    clips, values = parts[0].shape
    shapes = [(k * clips, values // 2) for k in (len(parts), len(parts) - 1)]
    return pl.pallas_call(
        stack_kernel,
        out_shape=[jax.ShapeDtypeStruct(x, BF16) for x in shapes],
        in_specs=[VMEM] * len(parts),
        out_specs=[VMEM] * 2,
        compiler_params=params(),
        cost_estimate=cost(3),
        name="stack",
    )(*parts)


def flip(n, bit):
    return [(i, i ^ bit) for i in range(n)]


def on_device(n, latents, noise, offsets, times, embed):
    clips = latents.shape[0]

    def core(x):
        return lax.ppermute(x, "clip", flip(n, 1))

    def across(x):
        return lax.ppermute(x, "clip", flip(n, 2))

    def along(x, k):
        return lax.ppermute(x, "clip", flip(n, 4 * k))

    def other_val(x):
        return lax.ppermute(x, "val", [(0, 1), (1, 0)])

    def other_both(x):
        pairs = [(2 * i + v, 2 * (i ^ 2) + 1 - v) for i in range(n) for v in range(2)]
        return lax.ppermute(x, ("clip", "val"), pairs)

    def beside(*x):
        return jnp.concatenate(x, axis=1)

    def below(*x):
        return jnp.concatenate(x, axis=0)

    own = split_frames(noise, offsets)
    cut = own.shape[1] // 2
    noi = [own]
    noi.append(along(own, 1))
    noi.append(along(own, 2))
    noi.append(along(noi[2], 1))
    keep = [x[:, :cut] for x in noi]
    send = [x[:, cut:] for x in noi]
    times, embed, latents, _ = lax.optimization_barrier((times, embed, latents, own))
    table, column, lat = stage(times, embed, latents)
    own_late, lat = lax.optimization_barrier((own, lat))
    got_own = other_val(below(own_late[:, cut:], lat[:, cut:]))
    lat_far, _ = lax.optimization_barrier((across(lat), noi[2]))
    lat_core = core(below(lat, lat_far))
    part = gram_block(clips, lat, lat_far, lat_core, *noi)
    got_x, got_v, got_b = across(part), other_val(part), other_both(part)
    own_late, _ = lax.optimization_barrier((own, lat_far))
    to_far, to_val = stack([own_late, *noi[1:3]])
    got_mid, far = other_val(to_val), across(to_far)
    got_last = other_val(send[3])
    got_own, got_mid, far, got_x = lax.optimization_barrier((got_own, got_mid, far, got_x))
    got, lat_got = below(got_own[:clips], got_mid, got_last), got_own[clips:]
    far_rest = across(below(keep[3], got))
    pair = below(part + got_v, got_x + got_b)
    rows = [along(pair, k) for k in (1, 2, 3)]
    far_rest, *rows = lax.optimization_barrier([far_rest] + rows)
    mine = below(pair, *rows)
    line = below(*keep)
    beside_core = [core(x) for x in (line, got, far)]
    other = core(mine)
    weights = plan(mine, other, clips)
    parts = [line, beside_core[0], got, beside_core[1]]
    parts += [far, beside_core[2], far_rest, core(far_rest)]
    first, second = [], []
    for k in (0, 1):
        first += [(k, s * clips) for s in range(4)]
        second += [(2 + k, s * clips) for s in range(4)]
    for k in (0, 1):
        first += [(4 + k, s * clips) for s in range(3)] + [(6 + k, 0)]
        second += [(6 + k, s * clips) for s in range(1, 5)]
    out = finish(column, weights, lat, lat_got, table, parts, (first, second))
    return out.reshape(clips, FRAME, out.shape[1])


def warp_and_gather(latents, noise, offsets, times, embed):
    clips = latents.shape[0]
    warped = warp_noise(noise, offsets)
    panel = lax.all_gather(warped, "clip", axis=0, tiled=True)
    gram = lax.dot_general(latents, panel, NT, preferred_element_type=F32)
    square = jnp.sum(jnp.square(panel.astype(F32)), axis=1)
    part = lax.psum(square[None, :] - 2.0 * gram, "val")
    full = lax.all_gather(part, "clip", axis=0, tiled=True) * (-SCALE)
    share, right = sinkhorn(full)
    own = lax.dynamic_slice_in_dim(share, lax.axis_index("clip") * clips, clips, axis=0)
    weights = softmax_rows(own, right).astype(BF16)
    coupled = jnp.dot(weights, panel, preferred_element_type=F32)
    t = times[:, None]
    mixed = ((1.0 - t) * latents.astype(F32) + t * coupled).astype(BF16)
    cube = mixed.reshape(clips, latents.shape[1] // S, S)
    cube = lax.all_to_all(cube, "val", split_axis=2, concat_axis=1, tiled=True)
    return jnp.einsum("cps,pd->csd", cube, embed, preferred_element_type=F32).astype(BF16)


def solution(mesh):
    n, v = mesh.shape["clip"], mesh.shape["val"]
    body = functools.partial(on_device, n) if (n, v) == (16, 2) else warp_and_gather
    placed = (P("clip", "val"), P("clip", "val"), P("clip", None, None), P("clip"), P())
    return jax.shard_map(
        body, mesh=mesh, in_specs=placed, out_specs=P("clip", "val", None), check_vma=False
    )
```

```python
import functools
import math

import jax
import jax.numpy as jnp
from jax import lax
from jax.experimental import pallas as pl
from jax.experimental.pallas import tpu as pltpu
from jax.sharding import PartitionSpec as P

P_SIZE = 64
D = 5120
FR = 2
GW = 16
GH = 4
ITERS = 4
S = 128
FRAME = GW * GH
SCALE = 2.0 / math.sqrt(P_SIZE * S)
NT = (((1,), (1,)), ((), ()))
TN = (((0,), (0,)), ((), ()))
F32 = jnp.float32
BF16 = jnp.bfloat16
HBM = pl.BlockSpec(memory_space=pltpu.HBM)
VMEM = pl.BlockSpec(memory_space=pltpu.VMEM)
SMEM = pl.BlockSpec(memory_space=pltpu.SMEM)


def params(mib=48):
    return pltpu.CompilerParams(vmem_limit_bytes=mib * 1024 * 1024)


def cost(us):
    return pl.CostEstimate(flops=0, bytes_accessed=us * 3_500_000, transcendentals=0)


def lane_sources(offsets, frame, token, clips):
    square = (clips, clips)
    eye = lax.broadcasted_iota(jnp.int32, square, 0) == lax.broadcasted_iota(jnp.int32, square, 1)

    def column(k):
        spread = jnp.where(eye, jnp.broadcast_to(offsets[k : k + 1, :], square), 0)
        return jnp.sum(spread, axis=1, keepdims=True)

    shift_y = jnp.where(frame == 0, column(0), column(2))
    shift_x = jnp.where(frame == 0, column(1), column(3))
    src_row = ((token // GW) - shift_y) & (GH - 1)
    src_col = (token - shift_x) & (GW - 1)
    return frame * FRAME + src_row * GW + src_col


def gather_lanes(tile, source):
    return jnp.take_along_axis(tile, source, axis=1, mode="promise_in_bounds")


def warp_kernel(offsets, noise, out):
    clips, values = noise.shape
    lane = lax.broadcasted_iota(jnp.int32, (clips, S), 1)
    source = lane_sources(offsets, lane // FRAME, lane % FRAME, clips)
    for p in range(values // S):
        cut = slice(p * S, (p + 1) * S)
        out[:, cut] = gather_lanes(noise[:, cut].astype(F32), source).astype(BF16)


def flat_offsets(offsets):
    return offsets.transpose(1, 2, 0).reshape(FR * 2, offsets.shape[0])


def warp_noise(noise, offsets):
    return pl.pallas_call(
        warp_kernel,
        out_shape=jax.ShapeDtypeStruct(noise.shape, BF16),
        in_specs=[VMEM, VMEM],
        out_specs=VMEM,
        compiler_params=params(),
        name="warp",
    )(flat_offsets(offsets), noise)


def warp_frame(offsets, noise, frame, out):
    clips, values = noise.shape
    half = values // S // 2
    lane = lax.broadcasted_iota(jnp.int32, (clips, S), 1)
    low = lane < FRAME
    source = lane_sources(offsets, frame + lane * 0, lane % FRAME, clips)
    for q in range(half):
        near, far = slice(q * S, (q + 1) * S), slice((q + half) * S, (q + half + 1) * S)
        a, b = noise[:, near].astype(F32), noise[:, far].astype(F32)
        out[:, near] = jnp.where(low, gather_lanes(a, source), gather_lanes(b, source)).astype(BF16)


def take_frame(latents, frame, out):
    clips, values = latents.shape
    half = values // S // 2
    low = lax.broadcasted_iota(jnp.int32, (clips, S), 1) < FRAME
    for q in range(half):
        near, far = slice(q * S, (q + 1) * S), slice((q + half) * S, (q + half + 1) * S)
        a, b = latents[:, near].astype(F32), latents[:, far].astype(F32)
        first = jnp.where(low, a, pltpu.roll(b, FRAME, 1))
        second = jnp.where(low, pltpu.roll(a, FRAME, 1), b)
        out[:, near] = jnp.where(frame == 0, first, second).astype(BF16)


def split_kernel(offsets_in, noise_in, noise_out, offsets, noise, sems):
    small = pltpu.make_async_copy(offsets_in, offsets, sems.at[0])
    small.start()
    clips, values = noise.shape
    cut = values // 2
    pieces = 4
    step = cut // pieces
    loads = []
    for k in range(pieces):
        for h in range(2):
            here = (slice(None), pl.ds(h * cut + k * step, step))
            loads.append(pltpu.make_async_copy(noise_in.at[here], noise.at[here], sems.at[1 + 2 * k + h]))
            loads[-1].start()
    val = lax.axis_index("val")
    small.wait()
    lane = lax.broadcasted_iota(jnp.int32, (clips, S), 1)
    low = lane < FRAME
    sources = [lane_sources(offsets, f + lane * 0, lane % FRAME, clips) for f in (val, 1 - val)]
    for k in range(pieces):
        loads[2 * k].wait()
        loads[2 * k + 1].wait()
        for at in range(k * step, (k + 1) * step, S):
            near, far = slice(at, at + S), slice(cut + at, cut + at + S)
            a, b = noise[:, near].astype(F32), noise[:, far].astype(F32)
            for source, place in zip(sources, (near, far)):
                moved = jnp.where(low, gather_lanes(a, source), gather_lanes(b, source))
                noise_out[:, place] = moved.astype(BF16)


def in_hbm(x):
    return pltpu.with_memory_space_constraint(x, pltpu.HBM)


def split_frames(noise, offsets):
    inputs = [flat_offsets(offsets), noise]
    return pl.pallas_call(
        split_kernel,
        out_shape=jax.ShapeDtypeStruct(noise.shape, BF16),
        in_specs=[HBM] * 2,
        out_specs=VMEM,
        scratch_shapes=[pltpu.VMEM(x.shape, x.dtype) for x in inputs]
        + [pltpu.SemaphoreType.DMA((9,))],
        compiler_params=params(),
        name="split",
    )(*map(in_hbm, inputs))


def stage_kernel(times_in, embed, latents_in, table, column, lat, times, latents, sems):
    small = pltpu.make_async_copy(times_in, times, sems.at[0])
    load = pltpu.make_async_copy(latents_in, latents, sems.at[1])
    large = pltpu.make_async_copy(embed, table, sems.at[2])
    for copy in (small, load, large):
        copy.start()
    val = lax.axis_index("val")
    clips, lanes = column.shape
    row = lax.broadcasted_iota(jnp.int32, (clips, lanes), 0)
    t = jnp.zeros((clips, lanes), F32)
    small.wait()
    for i in range(clips):
        t = jnp.where(row == i, times[i], t)
    column[...] = t
    cut = latents.shape[1] // 2
    load.wait()
    take_frame(latents, val, lat.at[:, :cut])
    take_frame(latents, 1 - val, lat.at[:, cut:])
    large.wait()


def stage(times, embed, latents):
    return pl.pallas_call(
        stage_kernel,
        out_shape=[
            jax.ShapeDtypeStruct(embed.shape, BF16),
            jax.ShapeDtypeStruct((times.shape[0], 128), F32),
            jax.ShapeDtypeStruct(latents.shape, BF16),
        ],
        in_specs=[HBM] * 3,
        out_specs=[VMEM] * 3,
        scratch_shapes=[
            pltpu.SMEM(times.shape, F32),
            pltpu.VMEM(latents.shape, BF16),
            pltpu.SemaphoreType.DMA((3,)),
        ],
        compiler_params=params(),
        cost_estimate=cost(1),
        name="stage",
    )(*map(in_hbm, (times, embed, latents)))


def swap_groups(x, a, clips):
    lane = lax.broadcasted_iota(jnp.int32, x.shape, 1)
    for bit in (1, 2):
        w = bit * clips
        moved = jnp.where(lane & w == 0, pltpu.roll(x, x.shape[1] - w, 1), pltpu.roll(x, w, 1))
        x = jnp.where(a & bit == 0, x, moved)
    return x


def gram_kernel(clips, lat, lat_far, lat_core, *refs):
    place = lax.axis_index("clip")
    a, x, c = place // 4, (place // 2) % 2, place % 2
    rows = 4 * clips
    out = refs[-1]
    noi = jnp.concatenate([r[...] for r in refs[:-1]], axis=0)
    cols = noi.shape[0]
    left = jnp.concatenate([lat[...], lat_far[...], lat_core[...], noi], axis=0)
    prod = lax.dot_general(left, noi, NT, preferred_element_type=F32)
    square = (cols, cols)
    eye = lax.broadcasted_iota(jnp.int32, square, 0) == lax.broadcasted_iota(jnp.int32, square, 1)
    norm = jnp.sum(jnp.where(eye, prod[rows:], 0.0), axis=0, keepdims=True)
    part = norm - 2.0 * prod[:rows]
    blocks = [part[k * clips : (k + 1) * clips] for k in range(4)]
    near0 = jnp.where(c == 0, blocks[0], blocks[2])
    near1 = jnp.where(c == 0, blocks[2], blocks[0])
    far0 = jnp.where(c == 0, blocks[1], blocks[3])
    far1 = jnp.where(c == 0, blocks[3], blocks[1])
    near = jnp.concatenate([near0, near1], axis=0)
    far = jnp.concatenate([far0, far1], axis=0)
    packed = jnp.concatenate([jnp.where(x == 0, near, far), jnp.where(x == 0, far, near)], axis=1)
    out[...] = swap_groups(packed, a, clips)


def gram_block(clips, *args):
    return pl.pallas_call(
        functools.partial(gram_kernel, clips),
        out_shape=jax.ShapeDtypeStruct((2 * clips, 128), F32),
        in_specs=[VMEM] * len(args),
        out_specs=VMEM,
        compiler_params=params(),
        cost_estimate=cost(5),
        name="gram",
    )(*args)


def sinkhorn(kernel):
    top = jnp.max(kernel, axis=1, keepdims=True)
    row = top + jnp.log(jnp.sum(jnp.exp(kernel - top), axis=1, keepdims=True))
    u = kernel - row
    top = jnp.max(u, axis=0, keepdims=True)
    share = jnp.exp(u - top)
    right = 1.0 / jnp.sum(share, axis=0, keepdims=True)
    for _ in range(ITERS - 1):
        left = 1.0 / jnp.sum(share * right, axis=1, keepdims=True)
        right = 1.0 / jnp.sum(share * left, axis=0, keepdims=True)
    return share, right


def softmax_rows(share, right):
    e = share * right
    return e / jnp.sum(e, axis=1, keepdims=True)


def plan_kernel(clips, mine, other, out, full):
    place = lax.axis_index("clip")
    a, b = place // 4, place % 4
    half = 2 * clips
    low = lax.broadcasted_iota(jnp.int32, (half, 128), 1) < 64
    for s in range(mine.shape[0] // (2 * half)):
        for x in range(2):
            r = s * 2 * half
            g = mine[r + x * half : r + (x + 1) * half, :] * (-SCALE)
            h = other[r + x * half : r + (x + 1) * half, :] * (-SCALE)
            lanes = slice(x * 128, (x + 1) * 128)
            full[r : r + half, lanes] = jnp.where(low, g, pltpu.roll(h, 64, 1))
            full[r + half : r + 2 * half, lanes] = jnp.where(low, pltpu.roll(g, 64, 1), h)
    share, right = sinkhorn(full[...])
    full[...] = share
    own = full[pl.ds(pl.multiple_of(b * clips, clips), clips), :]
    weights = softmax_rows(own, right)
    for x in range(2):
        lanes = slice(x * 128, (x + 1) * 128)
        out[:, lanes] = swap_groups(weights[:, lanes], a, clips).astype(BF16)


def plan(mine, other, clips):
    n = mine.shape[0]
    return pl.pallas_call(
        functools.partial(plan_kernel, clips),
        out_shape=jax.ShapeDtypeStruct((clips, n), BF16),
        in_specs=[VMEM] * 2,
        out_specs=VMEM,
        scratch_shapes=[pltpu.VMEM((n, n), F32)],
        compiler_params=params(),
        name="plan",
    )(mine, other)


def finish_kernel(clips, block, layout, column, weights, lat_keep, lat_got, table, *refs):
    parts = refs[:-4]
    out, cube, result, sems = refs[-4:]
    val = lax.axis_index("val")
    t = column[:, :1]
    w = weights[...]
    cut = lat_got.shape[1]
    step = 256
    for h, lat in enumerate((lat_keep, lat_got)):
        for at in range(0, cut, step):
            lanes = slice(at, at + step)
            panel = jnp.concatenate([parts[k][r : r + clips, lanes] for k, r in layout[h]], axis=0)
            coupled = jnp.dot(w, panel, preferred_element_type=F32)
            mixed = (1.0 - t) * lat[:, lanes].astype(F32) + t * coupled
            for q in range(step // S):
                cube[:, (h * cut + at) // S + q, :] = mixed[:, q * S : (q + 1) * S]
    values = 2 * cut
    tiles = values // S
    half = tiles // 2
    low = lax.broadcasted_iota(jnp.int32, (tiles, S), 1) < FRAME
    per_pair = 2 * FRAME // block
    steps = clips * FRAME // block

    def store(k):
        return pltpu.make_async_copy(result.at[k], out.at[pl.ds(k * block, block)], sems.at[k])

    for k in range(clips // 2):
        x, y = cube[2 * k], cube[2 * k + 1]
        near = jnp.where(low, x, pltpu.roll(y, FRAME, 1))
        far = jnp.where(low, pltpu.roll(x, FRAME, 1), y)
        mine = jnp.concatenate([near[:half], far[:half]], axis=0)
        other = jnp.concatenate([near[half:], far[half:]], axis=0)
        both = [jnp.where(val == 0, mine, other), jnp.where(val == 0, other, mine)]
        lhs = jnp.concatenate(both, axis=0).astype(BF16)
        for j in range(per_pair):
            step = k * per_pair + j
            tokens = lhs[:, j * block : (j + 1) * block]
            full = lax.dot_general(tokens, table[...], TN, preferred_element_type=F32)
            result[step] = full.astype(BF16)
            store(step).start()
    for k in range(steps):
        store(k).wait()


def finish(column, weights, lat_keep, lat_got, table, parts, layout, block=FRAME):
    clips, values = lat_keep.shape
    tokens, width = clips * FRAME, table.shape[1]
    return pl.pallas_call(
        functools.partial(finish_kernel, clips, block, layout),
        out_shape=jax.ShapeDtypeStruct((tokens, width), BF16),
        in_specs=[VMEM] * (5 + len(parts)),
        out_specs=HBM,
        scratch_shapes=[
            pltpu.VMEM((clips, values // S, S), F32),
            pltpu.VMEM((tokens // block, block, width), BF16),
            pltpu.SemaphoreType.DMA((tokens // block,)),
        ],
        compiler_params=params(),
        name="finish",
    )(column, weights, lat_keep, lat_got, table, *parts)


def stack_kernel(*refs):
    parts, (firsts, seconds) = refs[:-2], refs[-2:]
    clips, values = parts[0].shape
    cut = values // 2
    for k, part in enumerate(parts):
        firsts[k * clips : (k + 1) * clips, :] = part[:, :cut]
        if k:
            seconds[(k - 1) * clips : k * clips, :] = part[:, cut:]


def stack(parts):
    clips, values = parts[0].shape
    shapes = [(k * clips, values // 2) for k in (len(parts), len(parts) - 1)]
    return pl.pallas_call(
        stack_kernel,
        out_shape=[jax.ShapeDtypeStruct(x, BF16) for x in shapes],
        in_specs=[VMEM] * len(parts),
        out_specs=[VMEM] * 2,
        compiler_params=params(),
        cost_estimate=cost(3),
        name="stack",
    )(*parts)


def flip(n, bit):
    return [(i, i ^ bit) for i in range(n)]


def on_device(n, latents, noise, offsets, times, embed):
    clips = latents.shape[0]

    def core(x):
        return lax.ppermute(x, "clip", flip(n, 1))

    def across(x):
        return lax.ppermute(x, "clip", flip(n, 2))

    def along(x, k):
        return lax.ppermute(x, "clip", flip(n, 4 * k))

    def other_val(x):
        return lax.ppermute(x, "val", [(0, 1), (1, 0)])

    def other_both(x):
        pairs = [(2 * i + v, 2 * (i ^ 2) + 1 - v) for i in range(n) for v in range(2)]
        return lax.ppermute(x, ("clip", "val"), pairs)

    def beside(*x):
        return jnp.concatenate(x, axis=1)

    def below(*x):
        return jnp.concatenate(x, axis=0)

    own = split_frames(noise, offsets)
    cut = own.shape[1] // 2
    noi = [own]
    noi.append(along(own, 1))
    noi.append(along(own, 2))
    noi.append(along(noi[2], 1))
    keep = [x[:, :cut] for x in noi]
    send = [x[:, cut:] for x in noi]
    times, embed, latents, _ = lax.optimization_barrier((times, embed, latents, own))
    table, column, lat = stage(times, embed, latents)
    own_late, lat = lax.optimization_barrier((own, lat))
    got_own = other_val(below(own_late[:, cut:], lat[:, cut:]))
    lat_far, _ = lax.optimization_barrier((across(lat), noi[2]))
    lat_core = core(below(lat, lat_far))
    part = gram_block(clips, lat, lat_far, lat_core, *noi)
    got_x, got_v, got_b = across(part), other_val(part), other_both(part)
    own_late, _ = lax.optimization_barrier((own, lat_far))
    to_far, to_val = stack([own_late, *noi[1:3]])
    got_mid, far = other_val(to_val), across(to_far)
    got_last = other_val(send[3])
    got_own, got_mid, far, got_x = lax.optimization_barrier((got_own, got_mid, far, got_x))
    got, lat_got = below(got_own[:clips], got_mid, got_last), got_own[clips:]
    far_rest = across(below(keep[3], got))
    pair = below(part + got_v, got_x + got_b)
    rows = [along(pair, k) for k in (2, 1, 3)]
    far_rest, *rows = lax.optimization_barrier([far_rest] + rows)
    mine = below(pair, *rows)
    line = below(*keep)
    beside_core = [core(x) for x in (line, got, far)]
    other, *beside_core = lax.optimization_barrier([core(mine)] + beside_core)
    weights = plan(mine, other, clips)
    parts = [line, beside_core[0], got, beside_core[1]]
    parts += [far, beside_core[2], far_rest, core(far_rest)]
    first, second = [], []
    for k in (0, 1):
        first += [(k, s * clips) for s in range(4)]
        second += [(2 + k, s * clips) for s in range(4)]
    for k in (0, 1):
        first += [(4 + k, s * clips) for s in range(3)] + [(6 + k, 0)]
        second += [(6 + k, s * clips) for s in range(1, 5)]
    out = finish(column, weights, lat, lat_got, table, parts, (first, second))
    return out.reshape(clips, FRAME, out.shape[1])


def warp_and_gather(latents, noise, offsets, times, embed):
    clips = latents.shape[0]
    warped = warp_noise(noise, offsets)
    panel = lax.all_gather(warped, "clip", axis=0, tiled=True)
    gram = lax.dot_general(latents, panel, NT, preferred_element_type=F32)
    square = jnp.sum(jnp.square(panel.astype(F32)), axis=1)
    part = lax.psum(square[None, :] - 2.0 * gram, "val")
    full = lax.all_gather(part, "clip", axis=0, tiled=True) * (-SCALE)
    share, right = sinkhorn(full)
    own = lax.dynamic_slice_in_dim(share, lax.axis_index("clip") * clips, clips, axis=0)
    weights = softmax_rows(own, right).astype(BF16)
    coupled = jnp.dot(weights, panel, preferred_element_type=F32)
    t = times[:, None]
    mixed = ((1.0 - t) * latents.astype(F32) + t * coupled).astype(BF16)
    cube = mixed.reshape(clips, latents.shape[1] // S, S)
    cube = lax.all_to_all(cube, "val", split_axis=2, concat_axis=1, tiled=True)
    return jnp.einsum("cps,pd->csd", cube, embed, preferred_element_type=F32).astype(BF16)


def solution(mesh):
    n, v = mesh.shape["clip"], mesh.shape["val"]
    body = functools.partial(on_device, n) if (n, v) == (16, 2) else warp_and_gather
    placed = (P("clip", "val"), P("clip", "val"), P("clip", None, None), P("clip"), P())
    return jax.shard_map(
        body, mesh=mesh, in_specs=placed, out_specs=P("clip", "val", None), check_vma=False
    )
```

```python
import functools
import math

import jax
import jax.numpy as jnp
from jax import lax
from jax.experimental import pallas as pl
from jax.experimental.pallas import tpu as pltpu
from jax.sharding import PartitionSpec as P

P_SIZE = 64
D = 5120
FR = 2
GW = 16
GH = 4
ITERS = 4
S = 128
FRAME = GW * GH
SCALE = 2.0 / math.sqrt(P_SIZE * S)
NT = (((1,), (1,)), ((), ()))
TN = (((0,), (0,)), ((), ()))
F32 = jnp.float32
BF16 = jnp.bfloat16
HBM = pl.BlockSpec(memory_space=pltpu.HBM)
VMEM = pl.BlockSpec(memory_space=pltpu.VMEM)
SMEM = pl.BlockSpec(memory_space=pltpu.SMEM)


def params(mib=48):
    return pltpu.CompilerParams(vmem_limit_bytes=mib * 1024 * 1024)


def cost(us):
    return pl.CostEstimate(flops=0, bytes_accessed=us * 3_500_000, transcendentals=0)


def lane_sources(offsets, frame, token, clips):
    square = (clips, clips)
    eye = lax.broadcasted_iota(jnp.int32, square, 0) == lax.broadcasted_iota(jnp.int32, square, 1)

    def column(k):
        spread = jnp.where(eye, jnp.broadcast_to(offsets[k : k + 1, :], square), 0)
        return jnp.sum(spread, axis=1, keepdims=True)

    shift_y = jnp.where(frame == 0, column(0), column(2))
    shift_x = jnp.where(frame == 0, column(1), column(3))
    src_row = ((token // GW) - shift_y) & (GH - 1)
    src_col = (token - shift_x) & (GW - 1)
    return frame * FRAME + src_row * GW + src_col


def gather_lanes(tile, source):
    return jnp.take_along_axis(tile, source, axis=1, mode="promise_in_bounds")


def warp_kernel(offsets, noise, out):
    clips, values = noise.shape
    lane = lax.broadcasted_iota(jnp.int32, (clips, S), 1)
    source = lane_sources(offsets, lane // FRAME, lane % FRAME, clips)
    for p in range(values // S):
        cut = slice(p * S, (p + 1) * S)
        out[:, cut] = gather_lanes(noise[:, cut].astype(F32), source).astype(BF16)


def flat_offsets(offsets):
    return offsets.transpose(1, 2, 0).reshape(FR * 2, offsets.shape[0])


def warp_noise(noise, offsets):
    return pl.pallas_call(
        warp_kernel,
        out_shape=jax.ShapeDtypeStruct(noise.shape, BF16),
        in_specs=[VMEM, VMEM],
        out_specs=VMEM,
        compiler_params=params(),
        name="warp",
    )(flat_offsets(offsets), noise)


def warp_frame(offsets, noise, frame, out):
    clips, values = noise.shape
    half = values // S // 2
    lane = lax.broadcasted_iota(jnp.int32, (clips, S), 1)
    low = lane < FRAME
    source = lane_sources(offsets, frame + lane * 0, lane % FRAME, clips)
    for q in range(half):
        near, far = slice(q * S, (q + 1) * S), slice((q + half) * S, (q + half + 1) * S)
        a, b = noise[:, near].astype(F32), noise[:, far].astype(F32)
        out[:, near] = jnp.where(low, gather_lanes(a, source), gather_lanes(b, source)).astype(BF16)


def take_frame(latents, frame, out):
    clips, values = latents.shape
    half = values // S // 2
    low = lax.broadcasted_iota(jnp.int32, (clips, S), 1) < FRAME
    for q in range(half):
        near, far = slice(q * S, (q + 1) * S), slice((q + half) * S, (q + half + 1) * S)
        a, b = latents[:, near].astype(F32), latents[:, far].astype(F32)
        first = jnp.where(low, a, pltpu.roll(b, FRAME, 1))
        second = jnp.where(low, pltpu.roll(a, FRAME, 1), b)
        out[:, near] = jnp.where(frame == 0, first, second).astype(BF16)


def split_kernel(offsets_in, noise_in, noise_out, offsets, noise, sems):
    small = pltpu.make_async_copy(offsets_in, offsets, sems.at[0])
    small.start()
    clips, values = noise.shape
    cut = values // 2
    pieces = 4
    step = cut // pieces
    loads = []
    for k in range(pieces):
        for h in range(2):
            here = (slice(None), pl.ds(h * cut + k * step, step))
            loads.append(pltpu.make_async_copy(noise_in.at[here], noise.at[here], sems.at[1 + 2 * k + h]))
            loads[-1].start()
    val = lax.axis_index("val")
    small.wait()
    lane = lax.broadcasted_iota(jnp.int32, (clips, S), 1)
    low = lane < FRAME
    sources = [lane_sources(offsets, f + lane * 0, lane % FRAME, clips) for f in (val, 1 - val)]
    for k in range(pieces):
        loads[2 * k].wait()
        loads[2 * k + 1].wait()
        for at in range(k * step, (k + 1) * step, S):
            near, far = slice(at, at + S), slice(cut + at, cut + at + S)
            a, b = noise[:, near].astype(F32), noise[:, far].astype(F32)
            for source, place in zip(sources, (near, far)):
                moved = jnp.where(low, gather_lanes(a, source), gather_lanes(b, source))
                noise_out[:, place] = moved.astype(BF16)


def in_hbm(x):
    return pltpu.with_memory_space_constraint(x, pltpu.HBM)


def split_frames(noise, offsets):
    inputs = [flat_offsets(offsets), noise]
    return pl.pallas_call(
        split_kernel,
        out_shape=jax.ShapeDtypeStruct(noise.shape, BF16),
        in_specs=[HBM] * 2,
        out_specs=VMEM,
        scratch_shapes=[pltpu.VMEM(x.shape, x.dtype) for x in inputs]
        + [pltpu.SemaphoreType.DMA((9,))],
        compiler_params=params(),
        name="split",
    )(*map(in_hbm, inputs))


def stage_kernel(times_in, embed, latents_in, table, column, lat, times, latents, sems):
    small = pltpu.make_async_copy(times_in, times, sems.at[0])
    load = pltpu.make_async_copy(latents_in, latents, sems.at[1])
    large = pltpu.make_async_copy(embed, table, sems.at[2])
    for copy in (small, load, large):
        copy.start()
    val = lax.axis_index("val")
    clips, lanes = column.shape
    row = lax.broadcasted_iota(jnp.int32, (clips, lanes), 0)
    t = jnp.zeros((clips, lanes), F32)
    small.wait()
    for i in range(clips):
        t = jnp.where(row == i, times[i], t)
    column[...] = t
    cut = latents.shape[1] // 2
    load.wait()
    take_frame(latents, val, lat.at[:, :cut])
    take_frame(latents, 1 - val, lat.at[:, cut:])
    large.wait()


def stage(times, embed, latents):
    return pl.pallas_call(
        stage_kernel,
        out_shape=[
            jax.ShapeDtypeStruct(embed.shape, BF16),
            jax.ShapeDtypeStruct((times.shape[0], 128), F32),
            jax.ShapeDtypeStruct(latents.shape, BF16),
        ],
        in_specs=[HBM] * 3,
        out_specs=[VMEM] * 3,
        scratch_shapes=[
            pltpu.SMEM(times.shape, F32),
            pltpu.VMEM(latents.shape, BF16),
            pltpu.SemaphoreType.DMA((3,)),
        ],
        compiler_params=params(),
        cost_estimate=cost(1),
        name="stage",
    )(*map(in_hbm, (times, embed, latents)))


def swap_groups(x, a, clips):
    lane = lax.broadcasted_iota(jnp.int32, x.shape, 1)
    for bit in (1, 2):
        w = bit * clips
        moved = jnp.where(lane & w == 0, pltpu.roll(x, x.shape[1] - w, 1), pltpu.roll(x, w, 1))
        x = jnp.where(a & bit == 0, x, moved)
    return x


def gram_kernel(clips, lat, lat_far, lat_core, *refs):
    place = lax.axis_index("clip")
    a, x, c = place // 4, (place // 2) % 2, place % 2
    rows = 4 * clips
    out = refs[-1]
    noi = jnp.concatenate([r[...] for r in refs[:-1]], axis=0)
    cols = noi.shape[0]
    left = jnp.concatenate([lat[...], lat_far[...], lat_core[...], noi], axis=0)
    prod = lax.dot_general(left, noi, NT, preferred_element_type=F32)
    square = (cols, cols)
    eye = lax.broadcasted_iota(jnp.int32, square, 0) == lax.broadcasted_iota(jnp.int32, square, 1)
    norm = jnp.sum(jnp.where(eye, prod[rows:], 0.0), axis=0, keepdims=True)
    part = norm - 2.0 * prod[:rows]
    blocks = [part[k * clips : (k + 1) * clips] for k in range(4)]
    near0 = jnp.where(c == 0, blocks[0], blocks[2])
    near1 = jnp.where(c == 0, blocks[2], blocks[0])
    far0 = jnp.where(c == 0, blocks[1], blocks[3])
    far1 = jnp.where(c == 0, blocks[3], blocks[1])
    near = jnp.concatenate([near0, near1], axis=0)
    far = jnp.concatenate([far0, far1], axis=0)
    packed = jnp.concatenate([jnp.where(x == 0, near, far), jnp.where(x == 0, far, near)], axis=1)
    out[...] = swap_groups(packed, a, clips)


def gram_block(clips, *args):
    return pl.pallas_call(
        functools.partial(gram_kernel, clips),
        out_shape=jax.ShapeDtypeStruct((2 * clips, 128), F32),
        in_specs=[VMEM] * len(args),
        out_specs=VMEM,
        compiler_params=params(),
        cost_estimate=cost(5),
        name="gram",
    )(*args)


def sinkhorn(kernel):
    top = jnp.max(kernel, axis=1, keepdims=True)
    row = top + jnp.log(jnp.sum(jnp.exp(kernel - top), axis=1, keepdims=True))
    u = kernel - row
    top = jnp.max(u, axis=0, keepdims=True)
    share = jnp.exp(u - top)
    right = 1.0 / jnp.sum(share, axis=0, keepdims=True)
    for _ in range(ITERS - 1):
        left = 1.0 / jnp.sum(share * right, axis=1, keepdims=True)
        right = 1.0 / jnp.sum(share * left, axis=0, keepdims=True)
    return share, right


def softmax_rows(share, right):
    e = share * right
    return e / jnp.sum(e, axis=1, keepdims=True)


def plan_kernel(clips, mine, other, out, full):
    place = lax.axis_index("clip")
    a, b = place // 4, place % 4
    half = 2 * clips
    low = lax.broadcasted_iota(jnp.int32, (half, 128), 1) < 64
    for s in range(mine.shape[0] // (2 * half)):
        for x in range(2):
            r = s * 2 * half
            g = mine[r + x * half : r + (x + 1) * half, :] * (-SCALE)
            h = other[r + x * half : r + (x + 1) * half, :] * (-SCALE)
            lanes = slice(x * 128, (x + 1) * 128)
            full[r : r + half, lanes] = jnp.where(low, g, pltpu.roll(h, 64, 1))
            full[r + half : r + 2 * half, lanes] = jnp.where(low, pltpu.roll(g, 64, 1), h)
    share, right = sinkhorn(full[...])
    full[...] = share
    own = full[pl.ds(pl.multiple_of(b * clips, clips), clips), :]
    weights = softmax_rows(own, right)
    for x in range(2):
        lanes = slice(x * 128, (x + 1) * 128)
        out[:, lanes] = swap_groups(weights[:, lanes], a, clips).astype(BF16)


def plan(mine, other, clips):
    n = mine.shape[0]
    return pl.pallas_call(
        functools.partial(plan_kernel, clips),
        out_shape=jax.ShapeDtypeStruct((clips, n), BF16),
        in_specs=[VMEM] * 2,
        out_specs=VMEM,
        scratch_shapes=[pltpu.VMEM((n, n), F32)],
        compiler_params=params(),
        name="plan",
    )(mine, other)


def finish_kernel(clips, block, layout, column, weights, lat_keep, lat_got, table, *refs):
    parts = refs[:-4]
    out, cube, result, sems = refs[-4:]
    val = lax.axis_index("val")
    t = column[:, :1]
    w = weights[...]
    cut = lat_got.shape[1]
    step = 256
    for h, lat in enumerate((lat_keep, lat_got)):
        for at in range(0, cut, step):
            lanes = slice(at, at + step)
            panel = jnp.concatenate([parts[k][r : r + clips, lanes] for k, r in layout[h]], axis=0)
            coupled = jnp.dot(w, panel, preferred_element_type=F32)
            mixed = (1.0 - t) * lat[:, lanes].astype(F32) + t * coupled
            for q in range(step // S):
                cube[:, (h * cut + at) // S + q, :] = mixed[:, q * S : (q + 1) * S]
    values = 2 * cut
    tiles = values // S
    half = tiles // 2
    low = lax.broadcasted_iota(jnp.int32, (tiles, S), 1) < FRAME
    per_pair = 2 * FRAME // block
    steps = clips * FRAME // block

    def store(k):
        return pltpu.make_async_copy(result.at[k], out.at[pl.ds(k * block, block)], sems.at[k])

    for k in range(clips // 2):
        x, y = cube[2 * k], cube[2 * k + 1]
        near = jnp.where(low, x, pltpu.roll(y, FRAME, 1))
        far = jnp.where(low, pltpu.roll(x, FRAME, 1), y)
        mine = jnp.concatenate([near[:half], far[:half]], axis=0)
        other = jnp.concatenate([near[half:], far[half:]], axis=0)
        both = [jnp.where(val == 0, mine, other), jnp.where(val == 0, other, mine)]
        lhs = jnp.concatenate(both, axis=0).astype(BF16)
        for j in range(per_pair):
            step = k * per_pair + j
            tokens = lhs[:, j * block : (j + 1) * block]
            full = lax.dot_general(tokens, table[...], TN, preferred_element_type=F32)
            result[step] = full.astype(BF16)
            store(step).start()
    for k in range(steps):
        store(k).wait()


def finish(column, weights, lat_keep, lat_got, table, parts, layout, block=FRAME // 2):
    clips, values = lat_keep.shape
    tokens, width = clips * FRAME, table.shape[1]
    return pl.pallas_call(
        functools.partial(finish_kernel, clips, block, layout),
        out_shape=jax.ShapeDtypeStruct((tokens, width), BF16),
        in_specs=[VMEM] * (5 + len(parts)),
        out_specs=HBM,
        scratch_shapes=[
            pltpu.VMEM((clips, values // S, S), F32),
            pltpu.VMEM((tokens // block, block, width), BF16),
            pltpu.SemaphoreType.DMA((tokens // block,)),
        ],
        compiler_params=params(),
        name="finish",
    )(column, weights, lat_keep, lat_got, table, *parts)


def stack_kernel(*refs):
    parts, (firsts, seconds) = refs[:-2], refs[-2:]
    clips, values = parts[0].shape
    cut = values // 2
    for k, part in enumerate(parts):
        firsts[k * clips : (k + 1) * clips, :] = part[:, :cut]
        if k:
            seconds[(k - 1) * clips : k * clips, :] = part[:, cut:]


def stack(parts):
    clips, values = parts[0].shape
    shapes = [(k * clips, values // 2) for k in (len(parts), len(parts) - 1)]
    return pl.pallas_call(
        stack_kernel,
        out_shape=[jax.ShapeDtypeStruct(x, BF16) for x in shapes],
        in_specs=[VMEM] * len(parts),
        out_specs=[VMEM] * 2,
        compiler_params=params(),
        cost_estimate=cost(3),
        name="stack",
    )(*parts)


def flip(n, bit):
    return [(i, i ^ bit) for i in range(n)]


def on_device(n, latents, noise, offsets, times, embed):
    clips = latents.shape[0]

    def core(x):
        return lax.ppermute(x, "clip", flip(n, 1))

    def across(x):
        return lax.ppermute(x, "clip", flip(n, 2))

    def along(x, k):
        return lax.ppermute(x, "clip", flip(n, 4 * k))

    def other_val(x):
        return lax.ppermute(x, "val", [(0, 1), (1, 0)])

    def other_both(x):
        pairs = [(2 * i + v, 2 * (i ^ 2) + 1 - v) for i in range(n) for v in range(2)]
        return lax.ppermute(x, ("clip", "val"), pairs)

    def beside(*x):
        return jnp.concatenate(x, axis=1)

    def below(*x):
        return jnp.concatenate(x, axis=0)

    own = split_frames(noise, offsets)
    cut = own.shape[1] // 2
    noi = [own]
    noi.append(along(own, 1))
    noi.append(along(own, 2))
    noi.append(along(noi[2], 1))
    keep = [x[:, :cut] for x in noi]
    send = [x[:, cut:] for x in noi]
    times, embed, latents, _ = lax.optimization_barrier((times, embed, latents, own))
    table, column, lat = stage(times, embed, latents)
    own_late, lat = lax.optimization_barrier((own, lat))
    got_own = other_val(below(own_late[:, cut:], lat[:, cut:]))
    lat_far, _ = lax.optimization_barrier((across(lat), noi[2]))
    lat_core = core(below(lat, lat_far))
    part = gram_block(clips, lat, lat_far, lat_core, *noi)
    got_x, got_v, got_b = across(part), other_val(part), other_both(part)
    own_late, _ = lax.optimization_barrier((own, lat_far))
    to_far, to_val = stack([own_late, *noi[1:3]])
    got_mid, far = other_val(to_val), across(to_far)
    got_last = other_val(send[3])
    got_own, got_mid, far, got_x = lax.optimization_barrier((got_own, got_mid, far, got_x))
    got, lat_got = below(got_own[:clips], got_mid, got_last), got_own[clips:]
    far_rest = across(below(keep[3], got))
    pair = below(part + got_v, got_x + got_b)
    rows = [along(pair, k) for k in (2, 1, 3)]
    far_rest, *rows = lax.optimization_barrier([far_rest] + rows)
    mine = below(pair, *rows)
    line = below(*keep)
    more = below(got, far)
    beside_core = [core(x) for x in (line, more)]
    other, *beside_core = lax.optimization_barrier([core(mine)] + beside_core)
    weights = plan(mine, other, clips)
    r4 = 4 * clips
    parts = [line, beside_core[0], got, beside_core[1][:r4]]
    parts += [far, beside_core[1][r4:], far_rest, core(far_rest)]
    first, second = [], []
    for k in (0, 1):
        first += [(k, s * clips) for s in range(4)]
        second += [(2 + k, s * clips) for s in range(4)]
    for k in (0, 1):
        first += [(4 + k, s * clips) for s in range(3)] + [(6 + k, 0)]
        second += [(6 + k, s * clips) for s in range(1, 5)]
    out = finish(column, weights, lat, lat_got, table, parts, (first, second))
    return out.reshape(clips, FRAME, out.shape[1])


def warp_and_gather(latents, noise, offsets, times, embed):
    clips = latents.shape[0]
    warped = warp_noise(noise, offsets)
    panel = lax.all_gather(warped, "clip", axis=0, tiled=True)
    gram = lax.dot_general(latents, panel, NT, preferred_element_type=F32)
    square = jnp.sum(jnp.square(panel.astype(F32)), axis=1)
    part = lax.psum(square[None, :] - 2.0 * gram, "val")
    full = lax.all_gather(part, "clip", axis=0, tiled=True) * (-SCALE)
    share, right = sinkhorn(full)
    own = lax.dynamic_slice_in_dim(share, lax.axis_index("clip") * clips, clips, axis=0)
    weights = softmax_rows(own, right).astype(BF16)
    coupled = jnp.dot(weights, panel, preferred_element_type=F32)
    t = times[:, None]
    mixed = ((1.0 - t) * latents.astype(F32) + t * coupled).astype(BF16)
    cube = mixed.reshape(clips, latents.shape[1] // S, S)
    cube = lax.all_to_all(cube, "val", split_axis=2, concat_axis=1, tiled=True)
    return jnp.einsum("cps,pd->csd", cube, embed, preferred_element_type=F32).astype(BF16)


def solution(mesh):
    n, v = mesh.shape["clip"], mesh.shape["val"]
    body = functools.partial(on_device, n) if (n, v) == (16, 2) else warp_and_gather
    placed = (P("clip", "val"), P("clip", "val"), P("clip", None, None), P("clip"), P())
    return jax.shard_map(
        body, mesh=mesh, in_specs=placed, out_specs=P("clip", "val", None), check_vma=False
    )
```

```python
import functools
import math

import jax
import jax.numpy as jnp
from jax import lax
from jax.experimental import pallas as pl
from jax.experimental.pallas import tpu as pltpu
from jax.sharding import PartitionSpec as P

P_SIZE = 64
D = 5120
FR = 2
GW = 16
GH = 4
ITERS = 4
S = 128
FRAME = GW * GH
SCALE = 2.0 / math.sqrt(P_SIZE * S)
NT = (((1,), (1,)), ((), ()))
TN = (((0,), (0,)), ((), ()))
F32 = jnp.float32
BF16 = jnp.bfloat16
HBM = pl.BlockSpec(memory_space=pltpu.HBM)
VMEM = pl.BlockSpec(memory_space=pltpu.VMEM)
SMEM = pl.BlockSpec(memory_space=pltpu.SMEM)


def params(mib=48):
    return pltpu.CompilerParams(vmem_limit_bytes=mib * 1024 * 1024)


def cost(us):
    return pl.CostEstimate(flops=0, bytes_accessed=us * 3_500_000, transcendentals=0)


def lane_sources(offsets, frame, token, clips):
    square = (clips, clips)
    eye = lax.broadcasted_iota(jnp.int32, square, 0) == lax.broadcasted_iota(jnp.int32, square, 1)

    def column(k):
        spread = jnp.where(eye, jnp.broadcast_to(offsets[k : k + 1, :], square), 0)
        return jnp.sum(spread, axis=1, keepdims=True)

    shift_y = jnp.where(frame == 0, column(0), column(2))
    shift_x = jnp.where(frame == 0, column(1), column(3))
    src_row = ((token // GW) - shift_y) & (GH - 1)
    src_col = (token - shift_x) & (GW - 1)
    return frame * FRAME + src_row * GW + src_col


def gather_lanes(tile, source):
    return jnp.take_along_axis(tile, source, axis=1, mode="promise_in_bounds")


def warp_kernel(offsets, noise, out):
    clips, values = noise.shape
    lane = lax.broadcasted_iota(jnp.int32, (clips, S), 1)
    source = lane_sources(offsets, lane // FRAME, lane % FRAME, clips)
    for p in range(values // S):
        cut = slice(p * S, (p + 1) * S)
        out[:, cut] = gather_lanes(noise[:, cut].astype(F32), source).astype(BF16)


def flat_offsets(offsets):
    return offsets.transpose(1, 2, 0).reshape(FR * 2, offsets.shape[0])


def warp_noise(noise, offsets):
    return pl.pallas_call(
        warp_kernel,
        out_shape=jax.ShapeDtypeStruct(noise.shape, BF16),
        in_specs=[VMEM, VMEM],
        out_specs=VMEM,
        compiler_params=params(),
        name="warp",
    )(flat_offsets(offsets), noise)


def warp_frame(offsets, noise, frame, out):
    clips, values = noise.shape
    half = values // S // 2
    lane = lax.broadcasted_iota(jnp.int32, (clips, S), 1)
    low = lane < FRAME
    source = lane_sources(offsets, frame + lane * 0, lane % FRAME, clips)
    for q in range(half):
        near, far = slice(q * S, (q + 1) * S), slice((q + half) * S, (q + half + 1) * S)
        a, b = noise[:, near].astype(F32), noise[:, far].astype(F32)
        out[:, near] = jnp.where(low, gather_lanes(a, source), gather_lanes(b, source)).astype(BF16)


def take_frame(latents, frame, out):
    clips, values = latents.shape
    half = values // S // 2
    low = lax.broadcasted_iota(jnp.int32, (clips, S), 1) < FRAME
    for q in range(half):
        near, far = slice(q * S, (q + 1) * S), slice((q + half) * S, (q + half + 1) * S)
        a, b = latents[:, near].astype(F32), latents[:, far].astype(F32)
        first = jnp.where(low, a, pltpu.roll(b, FRAME, 1))
        second = jnp.where(low, pltpu.roll(a, FRAME, 1), b)
        out[:, near] = jnp.where(frame == 0, first, second).astype(BF16)


def split_kernel(offsets_in, noise_in, noise_out, offsets, noise, sems):
    small = pltpu.make_async_copy(offsets_in, offsets, sems.at[0])
    small.start()
    clips, values = noise.shape
    cut = values // 2
    pieces = 4
    step = cut // pieces
    loads = []
    for k in range(pieces):
        for h in range(2):
            here = (slice(None), pl.ds(h * cut + k * step, step))
            loads.append(pltpu.make_async_copy(noise_in.at[here], noise.at[here], sems.at[1 + 2 * k + h]))
            loads[-1].start()
    val = lax.axis_index("val")
    small.wait()
    lane = lax.broadcasted_iota(jnp.int32, (clips, S), 1)
    low = lane < FRAME
    sources = [lane_sources(offsets, f + lane * 0, lane % FRAME, clips) for f in (val, 1 - val)]
    for k in range(pieces):
        loads[2 * k].wait()
        loads[2 * k + 1].wait()
        for at in range(k * step, (k + 1) * step, S):
            near, far = slice(at, at + S), slice(cut + at, cut + at + S)
            a, b = noise[:, near].astype(F32), noise[:, far].astype(F32)
            for source, place in zip(sources, (near, far)):
                moved = jnp.where(low, gather_lanes(a, source), gather_lanes(b, source))
                noise_out[:, place] = moved.astype(BF16)


def in_hbm(x):
    return pltpu.with_memory_space_constraint(x, pltpu.HBM)


def split_frames(noise, offsets):
    inputs = [flat_offsets(offsets), noise]
    return pl.pallas_call(
        split_kernel,
        out_shape=jax.ShapeDtypeStruct(noise.shape, BF16),
        in_specs=[HBM] * 2,
        out_specs=VMEM,
        scratch_shapes=[pltpu.VMEM(x.shape, x.dtype) for x in inputs]
        + [pltpu.SemaphoreType.DMA((9,))],
        compiler_params=params(),
        name="split",
    )(*map(in_hbm, inputs))


def stage_kernel(times_in, embed, latents_in, table, column, lat, times, latents, sems):
    small = pltpu.make_async_copy(times_in, times, sems.at[0])
    load = pltpu.make_async_copy(latents_in, latents, sems.at[1])
    large = pltpu.make_async_copy(embed, table, sems.at[2])
    for copy in (small, load, large):
        copy.start()
    val = lax.axis_index("val")
    clips, lanes = column.shape
    row = lax.broadcasted_iota(jnp.int32, (clips, lanes), 0)
    t = jnp.zeros((clips, lanes), F32)
    small.wait()
    for i in range(clips):
        t = jnp.where(row == i, times[i], t)
    column[...] = t
    cut = latents.shape[1] // 2
    load.wait()
    take_frame(latents, val, lat.at[:, :cut])
    take_frame(latents, 1 - val, lat.at[:, cut:])
    large.wait()


def stage(times, embed, latents):
    return pl.pallas_call(
        stage_kernel,
        out_shape=[
            jax.ShapeDtypeStruct(embed.shape, BF16),
            jax.ShapeDtypeStruct((times.shape[0], 128), F32),
            jax.ShapeDtypeStruct(latents.shape, BF16),
        ],
        in_specs=[HBM] * 3,
        out_specs=[VMEM] * 3,
        scratch_shapes=[
            pltpu.SMEM(times.shape, F32),
            pltpu.VMEM(latents.shape, BF16),
            pltpu.SemaphoreType.DMA((3,)),
        ],
        compiler_params=params(),
        cost_estimate=cost(1),
        name="stage",
    )(*map(in_hbm, (times, embed, latents)))


def swap_groups(x, a, clips):
    lane = lax.broadcasted_iota(jnp.int32, x.shape, 1)
    for bit in (1, 2):
        w = bit * clips
        moved = jnp.where(lane & w == 0, pltpu.roll(x, x.shape[1] - w, 1), pltpu.roll(x, w, 1))
        x = jnp.where(a & bit == 0, x, moved)
    return x


def gram_kernel(clips, lat, lat_far, lat_core, *refs):
    place = lax.axis_index("clip")
    a, x, c = place // 4, (place // 2) % 2, place % 2
    rows = 4 * clips
    out = refs[-1]
    noi = jnp.concatenate([r[...] for r in refs[:-1]], axis=0)
    cols = noi.shape[0]
    left = jnp.concatenate([lat[...], lat_far[...], lat_core[...], noi], axis=0)
    prod = lax.dot_general(left, noi, NT, preferred_element_type=F32)
    square = (cols, cols)
    eye = lax.broadcasted_iota(jnp.int32, square, 0) == lax.broadcasted_iota(jnp.int32, square, 1)
    norm = jnp.sum(jnp.where(eye, prod[rows:], 0.0), axis=0, keepdims=True)
    part = norm - 2.0 * prod[:rows]
    blocks = [part[k * clips : (k + 1) * clips] for k in range(4)]
    near0 = jnp.where(c == 0, blocks[0], blocks[2])
    near1 = jnp.where(c == 0, blocks[2], blocks[0])
    far0 = jnp.where(c == 0, blocks[1], blocks[3])
    far1 = jnp.where(c == 0, blocks[3], blocks[1])
    near = jnp.concatenate([near0, near1], axis=0)
    far = jnp.concatenate([far0, far1], axis=0)
    packed = jnp.concatenate([jnp.where(x == 0, near, far), jnp.where(x == 0, far, near)], axis=1)
    out[...] = swap_groups(packed, a, clips)


def gram_block(clips, *args):
    return pl.pallas_call(
        functools.partial(gram_kernel, clips),
        out_shape=jax.ShapeDtypeStruct((2 * clips, 128), F32),
        in_specs=[VMEM] * len(args),
        out_specs=VMEM,
        compiler_params=params(),
        cost_estimate=cost(5),
        name="gram",
    )(*args)


def sinkhorn(kernel):
    top = jnp.max(kernel, axis=1, keepdims=True)
    row = top + jnp.log(jnp.sum(jnp.exp(kernel - top), axis=1, keepdims=True))
    u = kernel - row
    top = jnp.max(u, axis=0, keepdims=True)
    share = jnp.exp(u - top)
    right = 1.0 / jnp.sum(share, axis=0, keepdims=True)
    for _ in range(ITERS - 1):
        left = 1.0 / jnp.sum(share * right, axis=1, keepdims=True)
        right = 1.0 / jnp.sum(share * left, axis=0, keepdims=True)
    return share, right


def softmax_rows(share, right):
    e = share * right
    return e / jnp.sum(e, axis=1, keepdims=True)


def plan_kernel(clips, mine, other, out, full):
    place = lax.axis_index("clip")
    a, b = place // 4, place % 4
    half = 2 * clips
    low = lax.broadcasted_iota(jnp.int32, (half, 128), 1) < 64
    for s in range(mine.shape[0] // (2 * half)):
        for x in range(2):
            r = s * 2 * half
            g = mine[r + x * half : r + (x + 1) * half, :] * (-SCALE)
            h = other[r + x * half : r + (x + 1) * half, :] * (-SCALE)
            lanes = slice(x * 128, (x + 1) * 128)
            full[r : r + half, lanes] = jnp.where(low, g, pltpu.roll(h, 64, 1))
            full[r + half : r + 2 * half, lanes] = jnp.where(low, pltpu.roll(g, 64, 1), h)
    share, right = sinkhorn(full[...])
    column = 4 * clips
    full[:column, :] = share[:column]
    own = full[pl.ds(pl.multiple_of(b * clips, clips), clips), :]
    weights = softmax_rows(own, right)
    for x in range(2):
        lanes = slice(x * 128, (x + 1) * 128)
        out[:, lanes] = swap_groups(weights[:, lanes], a, clips).astype(BF16)


def plan(mine, other, clips):
    n = mine.shape[0]
    return pl.pallas_call(
        functools.partial(plan_kernel, clips),
        out_shape=jax.ShapeDtypeStruct((clips, n), BF16),
        in_specs=[VMEM] * 2,
        out_specs=VMEM,
        scratch_shapes=[pltpu.VMEM((n, n), F32)],
        compiler_params=params(),
        name="plan",
    )(mine, other)


def finish_kernel(clips, block, layout, column, weights, lat_keep, lat_got, table, *refs):
    parts = refs[:-4]
    out, cube, result, sems = refs[-4:]
    val = lax.axis_index("val")
    t = column[:, :1]
    w = weights[...]
    cut = lat_got.shape[1]
    step = 256
    for h, lat in enumerate((lat_keep, lat_got)):
        for at in range(0, cut, step):
            lanes = slice(at, at + step)
            panel = jnp.concatenate([parts[k][r : r + clips, lanes] for k, r in layout[h]], axis=0)
            coupled = jnp.dot(w, panel, preferred_element_type=F32)
            mixed = (1.0 - t) * lat[:, lanes].astype(F32) + t * coupled
            for q in range(step // S):
                cube[:, (h * cut + at) // S + q, :] = mixed[:, q * S : (q + 1) * S]
    values = 2 * cut
    tiles = values // S
    half = tiles // 2
    low = lax.broadcasted_iota(jnp.int32, (tiles, S), 1) < FRAME
    per_pair = 2 * FRAME // block
    steps = clips * FRAME // block

    def store(k):
        return pltpu.make_async_copy(result.at[k], out.at[pl.ds(k * block, block)], sems.at[k])

    for k in range(clips // 2):
        x, y = cube[2 * k], cube[2 * k + 1]
        near = jnp.where(low, x, pltpu.roll(y, FRAME, 1))
        far = jnp.where(low, pltpu.roll(x, FRAME, 1), y)
        mine = jnp.concatenate([near[:half], far[:half]], axis=0)
        other = jnp.concatenate([near[half:], far[half:]], axis=0)
        both = [jnp.where(val == 0, mine, other), jnp.where(val == 0, other, mine)]
        lhs = jnp.concatenate(both, axis=0).astype(BF16)
        for j in range(per_pair):
            step = k * per_pair + j
            tokens = lhs[:, j * block : (j + 1) * block]
            full = lax.dot_general(tokens, table[...], TN, preferred_element_type=F32)
            result[step] = full.astype(BF16)
            store(step).start()
    for k in range(steps):
        store(k).wait()


def finish(column, weights, lat_keep, lat_got, table, parts, layout, block=FRAME):
    clips, values = lat_keep.shape
    tokens, width = clips * FRAME, table.shape[1]
    return pl.pallas_call(
        functools.partial(finish_kernel, clips, block, layout),
        out_shape=jax.ShapeDtypeStruct((tokens, width), BF16),
        in_specs=[VMEM] * (5 + len(parts)),
        out_specs=HBM,
        scratch_shapes=[
            pltpu.VMEM((clips, values // S, S), F32),
            pltpu.VMEM((tokens // block, block, width), BF16),
            pltpu.SemaphoreType.DMA((tokens // block,)),
        ],
        compiler_params=params(),
        name="finish",
    )(column, weights, lat_keep, lat_got, table, *parts)


def stack_kernel(*refs):
    parts, (firsts, seconds) = refs[:-2], refs[-2:]
    clips, values = parts[0].shape
    cut = values // 2
    for k, part in enumerate(parts):
        firsts[k * clips : (k + 1) * clips, :] = part[:, :cut]
        if k:
            seconds[(k - 1) * clips : k * clips, :] = part[:, cut:]


def stack(parts):
    clips, values = parts[0].shape
    shapes = [(k * clips, values // 2) for k in (len(parts), len(parts) - 1)]
    return pl.pallas_call(
        stack_kernel,
        out_shape=[jax.ShapeDtypeStruct(x, BF16) for x in shapes],
        in_specs=[VMEM] * len(parts),
        out_specs=[VMEM] * 2,
        compiler_params=params(),
        cost_estimate=cost(3),
        name="stack",
    )(*parts)


def flip(n, bit):
    return [(i, i ^ bit) for i in range(n)]


def on_device(n, latents, noise, offsets, times, embed):
    clips = latents.shape[0]

    def core(x):
        return lax.ppermute(x, "clip", flip(n, 1))

    def across(x):
        return lax.ppermute(x, "clip", flip(n, 2))

    def along(x, k):
        return lax.ppermute(x, "clip", flip(n, 4 * k))

    def other_val(x):
        return lax.ppermute(x, "val", [(0, 1), (1, 0)])

    def other_both(x):
        pairs = [(2 * i + v, 2 * (i ^ 2) + 1 - v) for i in range(n) for v in range(2)]
        return lax.ppermute(x, ("clip", "val"), pairs)

    def beside(*x):
        return jnp.concatenate(x, axis=1)

    def below(*x):
        return jnp.concatenate(x, axis=0)

    own = split_frames(noise, offsets)
    cut = own.shape[1] // 2
    noi = [own]
    noi.append(along(own, 1))
    noi.append(along(own, 2))
    noi.append(along(noi[2], 1))
    keep = [x[:, :cut] for x in noi]
    send = [x[:, cut:] for x in noi]
    times, embed, latents, _ = lax.optimization_barrier((times, embed, latents, own))
    table, column, lat = stage(times, embed, latents)
    own_late, lat = lax.optimization_barrier((own, lat))
    got_own = other_val(below(own_late[:, cut:], lat[:, cut:]))
    lat_far, _ = lax.optimization_barrier((across(lat), noi[2]))
    lat_core = core(below(lat, lat_far))
    part = gram_block(clips, lat, lat_far, lat_core, *noi)
    got_x, got_v, got_b = across(part), other_val(part), other_both(part)
    own_late, _ = lax.optimization_barrier((own, lat_far))
    to_far, to_val = stack([own_late, *noi[1:3]])
    got_mid, far = other_val(to_val), across(to_far)
    got_last = other_val(send[3])
    got_own, got_mid, far, got_x = lax.optimization_barrier((got_own, got_mid, far, got_x))
    got, lat_got = below(got_own[:clips], got_mid, got_last), got_own[clips:]
    far_rest = across(below(keep[3], got))
    pair = below(part + got_v, got_x + got_b)
    rows = [along(pair, k) for k in (2, 1, 3)]
    far_rest, *rows = lax.optimization_barrier([far_rest] + rows)
    mine = below(pair, *rows)
    line = below(*keep)
    beside_core = [core(x) for x in (line, got, far)]
    other, *beside_core = lax.optimization_barrier([core(mine)] + beside_core)
    weights = plan(mine, other, clips)
    parts = [line, beside_core[0], got, beside_core[1]]
    parts += [far, beside_core[2], far_rest, core(far_rest)]
    first, second = [], []
    for k in (0, 1):
        first += [(k, s * clips) for s in range(4)]
        second += [(2 + k, s * clips) for s in range(4)]
    for k in (0, 1):
        first += [(4 + k, s * clips) for s in range(3)] + [(6 + k, 0)]
        second += [(6 + k, s * clips) for s in range(1, 5)]
    out = finish(column, weights, lat, lat_got, table, parts, (first, second))
    return out.reshape(clips, FRAME, out.shape[1])


def warp_and_gather(latents, noise, offsets, times, embed):
    clips = latents.shape[0]
    warped = warp_noise(noise, offsets)
    panel = lax.all_gather(warped, "clip", axis=0, tiled=True)
    gram = lax.dot_general(latents, panel, NT, preferred_element_type=F32)
    square = jnp.sum(jnp.square(panel.astype(F32)), axis=1)
    part = lax.psum(square[None, :] - 2.0 * gram, "val")
    full = lax.all_gather(part, "clip", axis=0, tiled=True) * (-SCALE)
    share, right = sinkhorn(full)
    own = lax.dynamic_slice_in_dim(share, lax.axis_index("clip") * clips, clips, axis=0)
    weights = softmax_rows(own, right).astype(BF16)
    coupled = jnp.dot(weights, panel, preferred_element_type=F32)
    t = times[:, None]
    mixed = ((1.0 - t) * latents.astype(F32) + t * coupled).astype(BF16)
    cube = mixed.reshape(clips, latents.shape[1] // S, S)
    cube = lax.all_to_all(cube, "val", split_axis=2, concat_axis=1, tiled=True)
    return jnp.einsum("cps,pd->csd", cube, embed, preferred_element_type=F32).astype(BF16)


def solution(mesh):
    n, v = mesh.shape["clip"], mesh.shape["val"]
    body = functools.partial(on_device, n) if (n, v) == (16, 2) else warp_and_gather
    placed = (P("clip", "val"), P("clip", "val"), P("clip", None, None), P("clip"), P())
    return jax.shard_map(
        body, mesh=mesh, in_specs=placed, out_specs=P("clip", "val", None), check_vma=False
    )
```

```python
import functools
import math

import jax
import jax.numpy as jnp
from jax import lax
from jax.experimental import pallas as pl
from jax.experimental.pallas import tpu as pltpu
from jax.sharding import PartitionSpec as P

P_SIZE = 64
D = 5120
FR = 2
GW = 16
GH = 4
ITERS = 4
S = 128
FRAME = GW * GH
SCALE = 2.0 / math.sqrt(P_SIZE * S)
NT = (((1,), (1,)), ((), ()))
TN = (((0,), (0,)), ((), ()))
F32 = jnp.float32
BF16 = jnp.bfloat16
HBM = pl.BlockSpec(memory_space=pltpu.HBM)
VMEM = pl.BlockSpec(memory_space=pltpu.VMEM)
SMEM = pl.BlockSpec(memory_space=pltpu.SMEM)


def params(mib=48):
    return pltpu.CompilerParams(vmem_limit_bytes=mib * 1024 * 1024)


def cost(us):
    return pl.CostEstimate(flops=0, bytes_accessed=us * 3_500_000, transcendentals=0)


def lane_sources(offsets, frame, token, clips):
    square = (clips, clips)
    eye = lax.broadcasted_iota(jnp.int32, square, 0) == lax.broadcasted_iota(jnp.int32, square, 1)

    def column(k):
        spread = jnp.where(eye, jnp.broadcast_to(offsets[k : k + 1, :], square), 0)
        return jnp.sum(spread, axis=1, keepdims=True)

    shift_y = jnp.where(frame == 0, column(0), column(2))
    shift_x = jnp.where(frame == 0, column(1), column(3))
    src_row = ((token // GW) - shift_y) & (GH - 1)
    src_col = (token - shift_x) & (GW - 1)
    return frame * FRAME + src_row * GW + src_col


def gather_lanes(tile, source):
    return jnp.take_along_axis(tile, source, axis=1, mode="promise_in_bounds")


def warp_kernel(offsets, noise, out):
    clips, values = noise.shape
    lane = lax.broadcasted_iota(jnp.int32, (clips, S), 1)
    source = lane_sources(offsets, lane // FRAME, lane % FRAME, clips)
    for p in range(values // S):
        cut = slice(p * S, (p + 1) * S)
        out[:, cut] = gather_lanes(noise[:, cut].astype(F32), source).astype(BF16)


def flat_offsets(offsets):
    return offsets.transpose(1, 2, 0).reshape(FR * 2, offsets.shape[0])


def warp_noise(noise, offsets):
    return pl.pallas_call(
        warp_kernel,
        out_shape=jax.ShapeDtypeStruct(noise.shape, BF16),
        in_specs=[VMEM, VMEM],
        out_specs=VMEM,
        compiler_params=params(),
        name="warp",
    )(flat_offsets(offsets), noise)


def warp_frame(offsets, noise, frame, out):
    clips, values = noise.shape
    half = values // S // 2
    lane = lax.broadcasted_iota(jnp.int32, (clips, S), 1)
    low = lane < FRAME
    source = lane_sources(offsets, frame + lane * 0, lane % FRAME, clips)
    for q in range(half):
        near, far = slice(q * S, (q + 1) * S), slice((q + half) * S, (q + half + 1) * S)
        a, b = noise[:, near].astype(F32), noise[:, far].astype(F32)
        out[:, near] = jnp.where(low, gather_lanes(a, source), gather_lanes(b, source)).astype(BF16)


def take_frame(latents, frame, out):
    clips, values = latents.shape
    half = values // S // 2
    low = lax.broadcasted_iota(jnp.int32, (clips, S), 1) < FRAME
    for q in range(half):
        near, far = slice(q * S, (q + 1) * S), slice((q + half) * S, (q + half + 1) * S)
        a, b = latents[:, near].astype(F32), latents[:, far].astype(F32)
        first = jnp.where(low, a, pltpu.roll(b, FRAME, 1))
        second = jnp.where(low, pltpu.roll(a, FRAME, 1), b)
        out[:, near] = jnp.where(frame == 0, first, second).astype(BF16)


def split_kernel(offsets_in, noise_in, noise_out, offsets, noise, sems):
    small = pltpu.make_async_copy(offsets_in, offsets, sems.at[0])
    small.start()
    clips, values = noise.shape
    cut = values // 2
    pieces = 4
    step = cut // pieces
    loads = []
    for k in range(pieces):
        for h in range(2):
            here = (slice(None), pl.ds(h * cut + k * step, step))
            loads.append(pltpu.make_async_copy(noise_in.at[here], noise.at[here], sems.at[1 + 2 * k + h]))
            loads[-1].start()
    val = lax.axis_index("val")
    small.wait()
    lane = lax.broadcasted_iota(jnp.int32, (clips, S), 1)
    low = lane < FRAME
    sources = [lane_sources(offsets, f + lane * 0, lane % FRAME, clips) for f in (val, 1 - val)]
    for k in range(pieces):
        loads[2 * k].wait()
        loads[2 * k + 1].wait()
        for at in range(k * step, (k + 1) * step, S):
            near, far = slice(at, at + S), slice(cut + at, cut + at + S)
            a, b = noise[:, near].astype(F32), noise[:, far].astype(F32)
            for source, place in zip(sources, (near, far)):
                moved = jnp.where(low, gather_lanes(a, source), gather_lanes(b, source))
                noise_out[:, place] = moved.astype(BF16)


def in_hbm(x):
    return pltpu.with_memory_space_constraint(x, pltpu.HBM)


def split_frames(noise, offsets):
    inputs = [flat_offsets(offsets), noise]
    return pl.pallas_call(
        split_kernel,
        out_shape=jax.ShapeDtypeStruct(noise.shape, BF16),
        in_specs=[HBM] * 2,
        out_specs=VMEM,
        scratch_shapes=[pltpu.VMEM(x.shape, x.dtype) for x in inputs]
        + [pltpu.SemaphoreType.DMA((9,))],
        compiler_params=params(),
        name="split",
    )(*map(in_hbm, inputs))


def stage_kernel(times_in, embed, latents_in, table, column, lat, times, latents, sems):
    small = pltpu.make_async_copy(times_in, times, sems.at[0])
    load = pltpu.make_async_copy(latents_in, latents, sems.at[1])
    large = pltpu.make_async_copy(embed, table, sems.at[2])
    for copy in (small, load, large):
        copy.start()
    val = lax.axis_index("val")
    clips, lanes = column.shape
    row = lax.broadcasted_iota(jnp.int32, (clips, lanes), 0)
    t = jnp.zeros((clips, lanes), F32)
    small.wait()
    for i in range(clips):
        t = jnp.where(row == i, times[i], t)
    column[...] = t
    cut = latents.shape[1] // 2
    load.wait()
    take_frame(latents, val, lat.at[:, :cut])
    take_frame(latents, 1 - val, lat.at[:, cut:])
    large.wait()


def stage(times, embed, latents):
    return pl.pallas_call(
        stage_kernel,
        out_shape=[
            jax.ShapeDtypeStruct(embed.shape, BF16),
            jax.ShapeDtypeStruct((times.shape[0], 128), F32),
            jax.ShapeDtypeStruct(latents.shape, BF16),
        ],
        in_specs=[HBM] * 3,
        out_specs=[VMEM] * 3,
        scratch_shapes=[
            pltpu.SMEM(times.shape, F32),
            pltpu.VMEM(latents.shape, BF16),
            pltpu.SemaphoreType.DMA((3,)),
        ],
        compiler_params=params(),
        cost_estimate=cost(1),
        name="stage",
    )(*map(in_hbm, (times, embed, latents)))


def swap_groups(x, a, clips):
    lane = lax.broadcasted_iota(jnp.int32, x.shape, 1)
    for bit in (1, 2):
        w = bit * clips
        moved = jnp.where(lane & w == 0, pltpu.roll(x, x.shape[1] - w, 1), pltpu.roll(x, w, 1))
        x = jnp.where(a & bit == 0, x, moved)
    return x


def gram_kernel(clips, lat, lat_far, lat_core, *refs):
    place = lax.axis_index("clip")
    a, x, c = place // 4, (place // 2) % 2, place % 2
    rows = 4 * clips
    out = refs[-1]
    noi = jnp.concatenate([r[...] for r in refs[:-1]], axis=0)
    cols = noi.shape[0]
    left = jnp.concatenate([lat[...], lat_far[...], lat_core[...], noi], axis=0)
    prod = lax.dot_general(left, noi, NT, preferred_element_type=F32)
    square = (cols, cols)
    eye = lax.broadcasted_iota(jnp.int32, square, 0) == lax.broadcasted_iota(jnp.int32, square, 1)
    norm = jnp.sum(jnp.where(eye, prod[rows:], 0.0), axis=0, keepdims=True)
    part = (2.0 * prod[:rows] - norm) * SCALE
    blocks = [part[k * clips : (k + 1) * clips] for k in range(4)]
    near0 = jnp.where(c == 0, blocks[0], blocks[2])
    near1 = jnp.where(c == 0, blocks[2], blocks[0])
    far0 = jnp.where(c == 0, blocks[1], blocks[3])
    far1 = jnp.where(c == 0, blocks[3], blocks[1])
    near = jnp.concatenate([near0, near1], axis=0)
    far = jnp.concatenate([far0, far1], axis=0)
    packed = jnp.concatenate([jnp.where(x == 0, near, far), jnp.where(x == 0, far, near)], axis=1)
    out[...] = swap_groups(packed, a, clips)


def gram_block(clips, *args):
    return pl.pallas_call(
        functools.partial(gram_kernel, clips),
        out_shape=jax.ShapeDtypeStruct((2 * clips, 128), F32),
        in_specs=[VMEM] * len(args),
        out_specs=VMEM,
        compiler_params=params(),
        cost_estimate=cost(5),
        name="gram",
    )(*args)


def sinkhorn(kernel):
    top = jnp.max(kernel, axis=1, keepdims=True)
    row = top + jnp.log(jnp.sum(jnp.exp(kernel - top), axis=1, keepdims=True))
    u = kernel - row
    top = jnp.max(u, axis=0, keepdims=True)
    share = jnp.exp(u - top)
    right = 1.0 / jnp.sum(share, axis=0, keepdims=True)
    for _ in range(ITERS - 1):
        left = 1.0 / jnp.sum(share * right, axis=1, keepdims=True)
        right = 1.0 / jnp.sum(share * left, axis=0, keepdims=True)
    return share, right


def softmax_rows(share, right):
    e = share * right
    return e / jnp.sum(e, axis=1, keepdims=True)


def plan_kernel(clips, mine, other, out, full):
    place = lax.axis_index("clip")
    a, b = place // 4, place % 4
    half = 2 * clips
    low = lax.broadcasted_iota(jnp.int32, (half, 128), 1) < 64
    for s in range(mine.shape[0] // (2 * half)):
        for x in range(2):
            r = s * 2 * half
            g = mine[r + x * half : r + (x + 1) * half, :]
            h = other[r + x * half : r + (x + 1) * half, :]
            lanes = slice(x * 128, (x + 1) * 128)
            full[r : r + half, lanes] = jnp.where(low, g, pltpu.roll(h, 64, 1))
            full[r + half : r + 2 * half, lanes] = jnp.where(low, pltpu.roll(g, 64, 1), h)
    share, right = sinkhorn(full[...])
    column = 4 * clips
    full[:column, :] = share[:column]
    own = full[pl.ds(pl.multiple_of(b * clips, clips), clips), :]
    weights = softmax_rows(own, right)
    for x in range(2):
        lanes = slice(x * 128, (x + 1) * 128)
        out[:, lanes] = swap_groups(weights[:, lanes], a, clips).astype(BF16)


def plan(mine, other, clips):
    n = mine.shape[0]
    return pl.pallas_call(
        functools.partial(plan_kernel, clips),
        out_shape=jax.ShapeDtypeStruct((clips, n), BF16),
        in_specs=[VMEM] * 2,
        out_specs=VMEM,
        scratch_shapes=[pltpu.VMEM((n, n), F32)],
        compiler_params=params(),
        name="plan",
    )(mine, other)


def finish_kernel(clips, block, layout, column, weights, lat_keep, lat_got, table, *refs):
    parts = refs[:-4]
    out, cube, result, sems = refs[-4:]
    val = lax.axis_index("val")
    t = column[:, :1]
    w = weights[...]
    cut = lat_got.shape[1]
    step = 256
    for h, lat in enumerate((lat_keep, lat_got)):
        for at in range(0, cut, step):
            lanes = slice(at, at + step)
            panel = jnp.concatenate([parts[k][r : r + clips, lanes] for k, r in layout[h]], axis=0)
            coupled = jnp.dot(w, panel, preferred_element_type=F32)
            mixed = (1.0 - t) * lat[:, lanes].astype(F32) + t * coupled
            for q in range(step // S):
                cube[:, (h * cut + at) // S + q, :] = mixed[:, q * S : (q + 1) * S]
    values = 2 * cut
    tiles = values // S
    half = tiles // 2
    low = lax.broadcasted_iota(jnp.int32, (tiles, S), 1) < FRAME
    per_pair = 2 * FRAME // block
    steps = clips * FRAME // block

    def store(k):
        return pltpu.make_async_copy(result.at[k], out.at[pl.ds(k * block, block)], sems.at[k])

    for k in range(clips // 2):
        x, y = cube[2 * k], cube[2 * k + 1]
        near = jnp.where(low, x, pltpu.roll(y, FRAME, 1))
        far = jnp.where(low, pltpu.roll(x, FRAME, 1), y)
        mine = jnp.concatenate([near[:half], far[:half]], axis=0)
        other = jnp.concatenate([near[half:], far[half:]], axis=0)
        both = [jnp.where(val == 0, mine, other), jnp.where(val == 0, other, mine)]
        lhs = jnp.concatenate(both, axis=0).astype(BF16)
        for j in range(per_pair):
            step = k * per_pair + j
            tokens = lhs[:, j * block : (j + 1) * block]
            full = lax.dot_general(tokens, table[...], TN, preferred_element_type=F32)
            result[step] = full.astype(BF16)
            store(step).start()
    for k in range(steps):
        store(k).wait()


def finish(column, weights, lat_keep, lat_got, table, parts, layout, block=FRAME):
    clips, values = lat_keep.shape
    tokens, width = clips * FRAME, table.shape[1]
    return pl.pallas_call(
        functools.partial(finish_kernel, clips, block, layout),
        out_shape=jax.ShapeDtypeStruct((tokens, width), BF16),
        in_specs=[VMEM] * (5 + len(parts)),
        out_specs=HBM,
        scratch_shapes=[
            pltpu.VMEM((clips, values // S, S), F32),
            pltpu.VMEM((tokens // block, block, width), BF16),
            pltpu.SemaphoreType.DMA((tokens // block,)),
        ],
        compiler_params=params(),
        name="finish",
    )(column, weights, lat_keep, lat_got, table, *parts)


def stack_kernel(*refs):
    parts, (firsts, seconds) = refs[:-2], refs[-2:]
    clips, values = parts[0].shape
    cut = values // 2
    for k, part in enumerate(parts):
        firsts[k * clips : (k + 1) * clips, :] = part[:, :cut]
        if k:
            seconds[(k - 1) * clips : k * clips, :] = part[:, cut:]


def stack(parts):
    clips, values = parts[0].shape
    shapes = [(k * clips, values // 2) for k in (len(parts), len(parts) - 1)]
    return pl.pallas_call(
        stack_kernel,
        out_shape=[jax.ShapeDtypeStruct(x, BF16) for x in shapes],
        in_specs=[VMEM] * len(parts),
        out_specs=[VMEM] * 2,
        compiler_params=params(),
        cost_estimate=cost(3),
        name="stack",
    )(*parts)


def flip(n, bit):
    return [(i, i ^ bit) for i in range(n)]


def on_device(n, latents, noise, offsets, times, embed):
    clips = latents.shape[0]

    def core(x):
        return lax.ppermute(x, "clip", flip(n, 1))

    def across(x):
        return lax.ppermute(x, "clip", flip(n, 2))

    def along(x, k):
        return lax.ppermute(x, "clip", flip(n, 4 * k))

    def other_val(x):
        return lax.ppermute(x, "val", [(0, 1), (1, 0)])

    def other_both(x):
        pairs = [(2 * i + v, 2 * (i ^ 2) + 1 - v) for i in range(n) for v in range(2)]
        return lax.ppermute(x, ("clip", "val"), pairs)

    def beside(*x):
        return jnp.concatenate(x, axis=1)

    def below(*x):
        return jnp.concatenate(x, axis=0)

    own = split_frames(noise, offsets)
    cut = own.shape[1] // 2
    noi = [own]
    noi.append(along(own, 1))
    noi.append(along(own, 2))
    noi.append(along(noi[2], 1))
    keep = [x[:, :cut] for x in noi]
    send = [x[:, cut:] for x in noi]
    times, embed, latents, _ = lax.optimization_barrier((times, embed, latents, own))
    table, column, lat = stage(times, embed, latents)
    own_late, lat = lax.optimization_barrier((own, lat))
    got_own = other_val(below(own_late[:, cut:], lat[:, cut:]))
    lat_far, _ = lax.optimization_barrier((across(lat), noi[2]))
    lat_core = core(below(lat, lat_far))
    part = gram_block(clips, lat, lat_far, lat_core, *noi)
    got_x, got_v, got_b = across(part), other_val(part), other_both(part)
    own_late, _ = lax.optimization_barrier((own, lat_far))
    to_far, to_val = stack([own_late, *noi[1:3]])
    got_mid, far = other_val(to_val), across(to_far)
    got_last = other_val(send[3])
    got_own, got_mid, far, got_x = lax.optimization_barrier((got_own, got_mid, far, got_x))
    got, lat_got = below(got_own[:clips], got_mid, got_last), got_own[clips:]
    far_rest = across(below(keep[3], got))
    pair = below(part + got_v, got_x + got_b)
    rows = [along(pair, k) for k in (2, 1, 3)]
    far_rest, *rows = lax.optimization_barrier([far_rest] + rows)
    mine = below(pair, *rows)
    line = below(*keep)
    beside_core = [core(x) for x in (line, got, far)]
    other, *beside_core = lax.optimization_barrier([core(mine)] + beside_core)
    weights = plan(mine, other, clips)
    parts = [line, beside_core[0], got, beside_core[1]]
    parts += [far, beside_core[2], far_rest, core(far_rest)]
    first, second = [], []
    for k in (0, 1):
        first += [(k, s * clips) for s in range(4)]
        second += [(2 + k, s * clips) for s in range(4)]
    for k in (0, 1):
        first += [(4 + k, s * clips) for s in range(3)] + [(6 + k, 0)]
        second += [(6 + k, s * clips) for s in range(1, 5)]
    out = finish(column, weights, lat, lat_got, table, parts, (first, second))
    return out.reshape(clips, FRAME, out.shape[1])


def warp_and_gather(latents, noise, offsets, times, embed):
    clips = latents.shape[0]
    warped = warp_noise(noise, offsets)
    panel = lax.all_gather(warped, "clip", axis=0, tiled=True)
    gram = lax.dot_general(latents, panel, NT, preferred_element_type=F32)
    square = jnp.sum(jnp.square(panel.astype(F32)), axis=1)
    part = lax.psum(square[None, :] - 2.0 * gram, "val")
    full = lax.all_gather(part, "clip", axis=0, tiled=True) * (-SCALE)
    share, right = sinkhorn(full)
    own = lax.dynamic_slice_in_dim(share, lax.axis_index("clip") * clips, clips, axis=0)
    weights = softmax_rows(own, right).astype(BF16)
    coupled = jnp.dot(weights, panel, preferred_element_type=F32)
    t = times[:, None]
    mixed = ((1.0 - t) * latents.astype(F32) + t * coupled).astype(BF16)
    cube = mixed.reshape(clips, latents.shape[1] // S, S)
    cube = lax.all_to_all(cube, "val", split_axis=2, concat_axis=1, tiled=True)
    return jnp.einsum("cps,pd->csd", cube, embed, preferred_element_type=F32).astype(BF16)


def solution(mesh):
    n, v = mesh.shape["clip"], mesh.shape["val"]
    body = functools.partial(on_device, n) if (n, v) == (16, 2) else warp_and_gather
    placed = (P("clip", "val"), P("clip", "val"), P("clip", None, None), P("clip"), P())
    return jax.shard_map(
        body, mesh=mesh, in_specs=placed, out_specs=P("clip", "val", None), check_vma=False
    )
```
